32 devices in a mesh: wn: 16 (over z, y, core), tile: 2 (over x).
Axes of the slice: x: 2, y: 2, z: 4, core: 2. Of those that a mesh axis runs over, the one named last changes fastest.
Arguments:
- divergence: float32 [2048, 128, 128], P('wn', 'tile'), may hold values from -6 to 6
- basis: bfloat16 [2048, 2048], P('wn'), may hold values from -0.125 to 0.125
- eigen: float32 [2048], P('wn'), may hold values from 0.1 to 4
- plane_level: int32 [2048], P('wn'), may hold values from 0 to 15
- spacing: float32 [16], replicated, may hold values from 0.3 to 3
- solid: int32 [128, 128], P('tile'), may hold values 0 or 1
Outputs:
- pressure: float32 [2048, 128, 128], P('wn', 'tile')
The draws below stay inside these ranges and needn't reach their ends.
All inputs are finite; a program needn't handle non-finite values. No bound on the sum of `solid` on one device may be relied on, other than what follows from the above.
Results may differ from the reference program's by a relative error of at most 0.0042.
Values may be sent and summed in bfloat16 or wider, within the bound.
No kernel may reach another device: no remote copies, remote signals or barrier semaphores. Data moves between devices by JAX's collectives and lax.ppermute only.
A program may use at most 64 MiB of HBM per device.

```python
import math
import jax
import jax.numpy as jnp
from jax import lax

NW = 2048
TZ = 128
SWEEPS = 4
LEVELS = 16
NX = 128


def plant(entries, rng, smallest, largest):
    longest = entries.shape.index(max(entries.shape))
    spots = []
    for shift in (0, 1):
        where = [jax.random.randint(jax.random.fold_in(rng, axis), (), 0, length) for axis, length in enumerate(entries.shape)]
        where[longest] = (where[longest] + shift) % entries.shape[longest]
        spots.append(tuple(where))
    return entries.at[spots[0]].set(smallest).at[spots[1]].set(largest)


def block_scale(own_key, shape, pieces, low, top_value):
    factor_of = 1.0
    for position, parts in pieces:
        draws = jax.random.uniform(jax.random.fold_in(jax.random.fold_in(own_key, 6), position), (parts,), jnp.float32, low / len(pieces), top_value / len(pieces))
        factor_of = factor_of * jnp.repeat(jnp.exp(draws), shape[position] // parts).reshape((-1,) + (1,) * (len(shape) - 1 - position))
    return factor_of


def centred(own_key, shape, deviation, reach, split=(), dtype=jnp.bfloat16):
    values = deviation * jax.random.normal(own_key, shape, jnp.float32)
    if split:
        values = values * block_scale(own_key, shape, split, -0.22, 0.18)
    return jnp.clip(values, -reach, reach).astype(dtype)


def setup_inputs(seed: int = 0) -> dict:
    key_of = jax.random.split(jax.random.key(seed), 7)
    return {
        "divergence": centred(key_of[0], (NW, NX, TZ), 1.0, 6.0, ((0, 16), (1, 2)), jnp.float32),
        "basis": centred(key_of[1], (NW, NW), NW ** -0.5, 0.125, ((0, 16),)),
        "eigen": jnp.clip(jnp.exp(math.log(4.0) - 3.6888794 * jax.random.uniform(key_of[2], (NW,), jnp.float32) ** block_scale(key_of[2], (NW,), ((0, 16),), -0.2, 0.2)), 0.1, 4.0),
        "plane_level": plant(jax.random.randint(key_of[3], (NW,), 0, LEVELS), jax.random.fold_in(key_of[3], 1), 0, LEVELS - 1).astype(jnp.int32),
        "spacing": jnp.clip(jnp.exp(jax.random.uniform(key_of[4], (LEVELS,), jnp.float32, math.log(0.3), math.log(3.0))), 0.3, 3.0),
        "solid": plant((jax.random.randint(key_of[5], (NX, TZ), 0, 5) < 1).astype(jnp.int32), jax.random.fold_in(key_of[5], 1), 0, 1),
    }


def helmholtz(block_rhs, block_eigen, fluid):
    diag = block_eigen[:, None, None] + 4.0
    spread = 4.0 / diag
    field = jnp.zeros(block_rhs.shape, jnp.float32)
    for step in range(SWEEPS):
        angle = math.cos(math.pi * (2 * step + 1) / (2 * SWEEPS))
        omega = 1.0 / (1.0 + spread * angle)
        beside = jnp.roll(field, 1, 1) + jnp.roll(field, -1, 1) + jnp.roll(field, 1, 2) + jnp.roll(field, -1, 2)
        remain = block_rhs - (diag * field - beside)
        field = fluid[None] * (field + omega * remain / diag)
    return field.astype(jnp.bfloat16)


def reference(divergence, basis, eigen, plane_level, spacing, solid):
    weight = spacing[plane_level]
    scaled = (weight[:, None, None] * divergence).astype(jnp.bfloat16)
    flat = scaled.reshape(NW, NX * TZ)
    spectral = jnp.dot(basis.T, flat, preferred_element_type=jnp.float32).astype(jnp.bfloat16)
    rhs = spectral.astype(jnp.float32).reshape(NW // 64, 64, NX, TZ)
    fluid = (1 - solid).astype(jnp.float32)
    blocks = eigen.reshape(NW // 64, 64)
    solved = lax.map(lambda pair: helmholtz(pair[0], pair[1], fluid), (rhs, blocks))
    solved = solved.reshape(NW, NX * TZ)
    pressure = jnp.dot(basis, solved, preferred_element_type=jnp.float32)
    return pressure.reshape(NW, NX, TZ)
```

```python
import functools
import math

import jax
import jax.numpy as jnp
from jax import lax
from jax.experimental import pallas as pl
from jax.experimental.pallas import tpu as pltpu
from jax.sharding import PartitionSpec as P

SWEEPS = 4
HALO = SWEEPS - 1
CHUNKS = 2
MIB = 1024 * 1024
F32, BF16 = jnp.float32, jnp.bfloat16


def params(mib):
    return pltpu.CompilerParams(vmem_limit_bytes=mib * MIB)


def cost(flops, nbytes):
    return pl.CostEstimate(flops=int(flops), bytes_accessed=int(nbytes), transcendentals=0)


def scale_body(table, w_ref, e_ref, x_ref, a_ref, b_ref):
    rows = x_ref.shape[1] // 2
    wide = x_ref.shape[2]
    swap = table[1] != 0
    w = w_ref[...]
    for r in range(rows):
        low = (x_ref[:, r, :] * w).T.astype(BF16)
        high = (x_ref[:, rows + r, :] * w).T.astype(BF16)
        a_ref[r * wide : (r + 1) * wide, :] = jnp.where(swap, high, low)
        b_ref[r * wide : (r + 1) * wide, :] = jnp.where(swap, low, high)
    a_ref[rows * wide :, :] = e_ref[...]
    b_ref[rows * wide :, :] = e_ref[...]


def scale_pair(table, weight, extra, divergence, rows):
    planes, _, wide = divergence.shape
    tall = rows * wide + extra.shape[0]
    out = jax.ShapeDtypeStruct((tall, planes), BF16)
    spec = pl.BlockSpec((tall, planes), lambda i, t: (0, 0))
    return pl.pallas_call(
        scale_body,
        grid_spec=pltpu.PrefetchScalarGridSpec(
            num_scalar_prefetch=1,
            grid=(1,),
            in_specs=[
                pl.BlockSpec((planes, 1), lambda i, t: (0, 0)),
                pl.BlockSpec(extra.shape, lambda i, t: (0, 0)),
                pl.BlockSpec((planes, 2 * rows, wide), lambda i, t: (0, t[0], 0)),
            ],
            out_specs=[spec, spec],
        ),
        out_shape=[out, out],
        compiler_params=params(12),
        cost_estimate=cost(planes * rows * wide * 2, planes * rows * wide * 12),
    )(table, weight, extra, divergence)


def place_body(table, *refs):
    a_ref, b_ref, o_ref = refs[0], refs[1], refs[-1]
    rows = o_ref.shape[1] // 2
    wide = o_ref.shape[2]
    swap = table[1] != 0
    for r in range(rows):
        a = a_ref[r * wide : (r + 1) * wide, :].astype(F32)
        b = b_ref[r * wide : (r + 1) * wide, :].astype(F32)
        o_ref[:, r, :] = jnp.where(swap, b, a).T
        o_ref[:, rows + r, :] = jnp.where(swap, a, b).T


def place_pair(table, a, b, out, shape, rows):
    planes, _, wide = shape
    spec = pl.BlockSpec((rows * wide, planes), lambda i, t: (0, 0))
    ins, specs, alias = [a, b], [spec, spec], {}
    if out is not None:
        ins.append(out)
        specs.append(pl.BlockSpec(memory_space=pl.ANY))
        alias = {3: 0}
    return pl.pallas_call(
        place_body,
        grid_spec=pltpu.PrefetchScalarGridSpec(
            num_scalar_prefetch=1,
            grid=(1,),
            in_specs=specs,
            out_specs=pl.BlockSpec((planes, 2 * rows, wide), lambda i, t: (0, t[0], 0)),
        ),
        out_shape=jax.ShapeDtypeStruct(shape, F32),
        input_output_aliases=alias,
        compiler_params=params(12),
        cost_estimate=cost(planes * rows * wide * 2, planes * rows * wide * 12),
    )(table, *ins)


def join_body(layout, blocks, planes, cells, half_ref, *refs):
    n, m = len(layout), len(blocks)
    b_refs, x_refs = refs[:n], refs[n : n + m]
    out_b, out_x, out_e, sem = refs[-4:]
    part = planes // 2
    half = half_ref[0]
    copies = []
    for ref, (kind, ids) in zip(b_refs, layout):
        for j, s in enumerate(ids):
            if kind == "whole":
                src, dst = ref, out_b.at[pl.ds(s * planes, planes), :]
            else:
                side = half if kind == "mine" else 1 - half
                start = pl.multiple_of(s * planes + side * part, part)
                src, dst = ref.at[pl.ds(j * part, part), :], out_b.at[pl.ds(start, part), :]
            copies.append((src, dst))
    for ref, s in zip(x_refs, blocks):
        tail = ref.shape[0] - cells
        copies.append((ref.at[pl.ds(cells, tail), :], out_e.at[s]))
        copies.append((ref.at[pl.ds(0, cells), :], out_x.at[s]))
    handles = [pltpu.make_async_copy(p, q, sem.at[k]) for k, (p, q) in enumerate(copies)]
    for h in handles:
        h.start()
    for h in handles:
        h.wait()


def join(half, pieces, layout, xs, blocks, shapes, held):
    planes, modes, cells, chips = shapes
    count = sum(len(ids) for _, ids in layout) + 2 * len(xs)
    out = [
        jax.ShapeDtypeStruct((chips * planes, modes), BF16),
        jax.ShapeDtypeStruct((chips, cells, planes), BF16),
        jax.ShapeDtypeStruct((chips, 16, planes), BF16),
    ]
    ins = [*pieces, *xs]
    anywhere = pl.BlockSpec(memory_space=pl.ANY)
    specs = [pl.BlockSpec(memory_space=pltpu.SMEM)] + [pl.BlockSpec(memory_space=pltpu.VMEM)] * len(ins)
    alias = {}
    if held is not None:
        alias = {1 + len(ins) + k: k for k in range(3)}
        specs += [anywhere] * 3
        ins += held
    return pl.pallas_call(
        functools.partial(join_body, layout, blocks, planes, cells),
        in_specs=specs,
        out_specs=[anywhere] * 3,
        out_shape=out,
        input_output_aliases=alias,
        scratch_shapes=[pltpu.SemaphoreType.DMA((count,))],
        compiler_params=params(12),
        cost_estimate=cost(0, 4 * sum(v.size for v in [*pieces, *xs])),
    )(half, *ins)


def forward_body(table, x_ref, b_ref, o_ref):
    x = jnp.concatenate([x_ref[k] for k in range(x_ref.shape[0])], axis=1)
    o_ref[...] = jnp.dot(x, b_ref[...], preferred_element_type=F32)


def forward(table, x, basis, modes, tile):
    chips, cells, planes = x.shape
    depth = chips * planes
    return pl.pallas_call(
        forward_body,
        grid_spec=pltpu.PrefetchScalarGridSpec(
            num_scalar_prefetch=1,
            grid=(modes // tile,),
            in_specs=[
                pl.BlockSpec((chips, cells, planes), lambda j, t: (0, 0, 0)),
                pl.BlockSpec((depth, tile), lambda j, t: (0, t[0] + j)),
            ],
            out_specs=pl.BlockSpec((cells, tile), lambda j, t: (0, j)),
        ),
        out_shape=jax.ShapeDtypeStruct((cells, modes), F32),
        compiler_params=params(20),
        cost_estimate=cost(2 * cells * depth * modes, 2 * cells * depth + 2 * depth * modes + 4 * cells * modes),
    )(table, x, basis)


def sweep_body(eigen_ref, fluid_ref, up_ref, own_ref, down_ref, o_ref, rhs, ua, ub):
    rows = own_ref.shape[0]
    ext = rows + 2 * HALO
    diag = eigen_ref[...] + 4.0
    spread = 4.0 / diag
    keep, gain = [], []
    for step in range(SWEEPS):
        omega = 1.0 / (1.0 + spread * math.cos(math.pi * (2 * step + 1) / (2 * SWEEPS)))
        keep.append(1.0 - omega)
        gain.append(omega / diag)

    def load(ref, first):
        def body(r, _):
            s = ref[r].astype(F32)
            rhs[first + r] = s
            ua[first + r] = fluid_ref[first + r] * (gain[0] * s)
            return 0

        lax.fori_loop(0, ref.shape[0], body, 0)

    load(up_ref, 0)
    load(own_ref, HALO)
    load(down_ref, HALO + rows)
    src, dst = ua, ub
    for step in range(1, SWEEPS):
        last = step == SWEEPS - 1

        def body(r, _, src=src, dst=dst, step=step, last=last):
            c = src[r]
            wide = c.shape[0]
            beside = src[r - 1] + src[r + 1] + (pltpu.roll(c, 1, 0) + pltpu.roll(c, wide - 1, 0))
            new = fluid_ref[r] * (keep[step] * c + gain[step] * (rhs[r] + beside))
            if last:
                o_ref[r - HALO] = new.astype(BF16)
            else:
                dst[r] = new
            return 0

        lax.fori_loop(step, ext - step, body, 0)
        src, dst = dst, src


def sweep(eigen, fluid, up, own, down):
    rows, wide, modes = own.shape
    ext, lanes = rows + 2 * HALO, 128
    block = lambda n: pl.BlockSpec((n, wide, lanes), lambda j: (0, 0, j))
    return pl.pallas_call(
        sweep_body,
        grid=(modes // lanes,),
        in_specs=[
            pl.BlockSpec((1, lanes), lambda j: (0, j)),
            pl.BlockSpec((ext, wide, lanes), lambda j: (0, 0, 0)),
            block(HALO),
            block(rows),
            block(HALO),
        ],
        out_specs=block(rows),
        out_shape=jax.ShapeDtypeStruct((rows, wide, modes), BF16),
        scratch_shapes=[pltpu.VMEM((ext, wide, lanes), F32)] * 3,
        compiler_params=params(16),
        cost_estimate=cost(modes * wide * ext * 400, 4 * modes * wide * ext),
    )(eigen, fluid, up, own, down)


def inverse_body(table, *refs):
    parts, b_ref, o_refs = refs[:-3], refs[-3], refs[-2:]
    wide = parts[0].shape[1]
    total = None
    for k, part in enumerate(parts):
        cols = pl.ds(pl.multiple_of(table[k] * wide, wide), wide)
        term = lax.dot_general(
            part[...], b_ref[:, cols], (((1,), (1,)), ((), ())), preferred_element_type=F32
        )
        total = term if total is None else total + term
    planes = b_ref.shape[0] // 2
    o_refs[0][...] = total[:, :planes].astype(BF16)
    o_refs[1][...] = total[:, planes:].astype(BF16)


def inverse(table, parts, basis, pair, planes):
    cells, wide = parts[0].shape
    modes = basis.shape[1]
    tile = min(cells, 512)
    out = jax.ShapeDtypeStruct((cells, planes), BF16)
    return pl.pallas_call(
        inverse_body,
        grid_spec=pltpu.PrefetchScalarGridSpec(
            num_scalar_prefetch=1,
            grid=(cells // tile,),
            in_specs=[pl.BlockSpec((tile, wide), lambda i, t: (i, 0))] * len(parts)
            + [pl.BlockSpec((2 * planes, modes), lambda i, t: (pair, 0))],
            out_specs=[pl.BlockSpec((tile, planes), lambda i, t: (i, 0))] * 2,
        ),
        out_shape=[out, out],
        compiler_params=params(20),
        cost_estimate=cost(4 * cells * modes * planes, 2 * cells * modes + 4 * planes * modes),
    )(table, *parts, basis)


def local(divergence, basis, eigen, plane_level, spacing, solid):
    planes, width, wide = divergence.shape
    wn, tiles = lax.axis_size("wn"), lax.axis_size("tile")
    chips = wn // 2
    rows = width // chips
    cells = rows * wide
    modes = basis.shape[1]
    mine = modes // 2
    me, t = lax.axis_index("wn"), lax.axis_index("tile")
    core, chip = me % 2, me // 2
    z, y, odd = chip // 2, chip % 2, t % 2
    i32 = lambda *v: jnp.stack([jnp.asarray(x, jnp.int32) for x in v])

    flip = lambda s: [(i, i ^ (2 * s)) for i in range(wn)]
    chip_swap = lambda v, s: lax.ppermute(v, "wn", flip(s))
    core_swap = lambda v: lax.ppermute(v, "wn", [(i, i ^ 1) for i in range(wn)])
    tile_swap = lambda v: lax.ppermute(v, "tile", [(i, i ^ 1) for i in range(tiles)])

    def pair_table(i):
        pz = z ^ i
        block = jnp.where(odd == 0, pz, chips // 2 - 1 - pz)
        return i32(block, y ^ (pz % 2) ^ odd)

    tables = [pair_table(i) for i in range(chips // 2)]
    order = lambda g: (g // 2) * 2 + ((g % 2) ^ ((g // 2) % 2))

    def device(tt, g):
        return order(g if tt % 2 == 0 else chips - 1 - g)

    snake = [(tt, device(tt, g)) for tt in range(tiles) for g in range(chips)]
    onward = [
        ((qa * 2 + c) * tiles + ta, (qb * 2 + c) * tiles + tb)
        for (ta, qa), (tb, qb) in zip(snake, snake[1:] + snake[:1])
        for c in range(2)
    ]
    backward = [(b, a) for a, b in onward]

    onehot = (plane_level[:, None] == jnp.arange(spacing.shape[0], dtype=jnp.int32)[None, :]).astype(F32)
    weight = jnp.sum(onehot * spacing[None, :], axis=1)[:, None]

    sibling = core_swap(eigen)
    both = jnp.stack([jnp.where(core == 0, eigen, sibling), jnp.where(core == 0, sibling, eigen)])
    high = lax.reduce_precision(both, 8, 7)
    middle = lax.reduce_precision(both - high, 8, 7)
    low = both - high - middle
    extra = jnp.concatenate([high, middle, low, jnp.zeros((10, planes), F32)]).astype(BF16)

    divergence = pltpu.with_memory_space_constraint(divergence, pltpu.HBM)
    send = [None] * chips
    for i in range(chips // 2):
        send[2 * i], send[2 * i + 1] = scale_pair(tables[i], weight, extra, divergence, rows)
    got = [send[0]] + [None] * (chips - 1)

    half = planes // 2
    steps = (chips // 2).bit_length()
    spread = list(range(1, chips))
    shares = [spread[k * len(spread) // steps : (k + 1) * len(spread) // steps] for k in range(steps)]
    if chips == 8:
        shares = [[1, 3, 5], [4, 6], [7, 2]]
    shares = [[]] + shares
    shapes = (planes, modes, cells, chips)
    state = {"held": None, "pieces": [(basis, ("whole", (0,)))], "blocks": [0]}

    def lay():
        pieces, blocks = state["pieces"], state["blocks"]
        state["pieces"], state["blocks"] = [], []
        state["held"] = join(
            i32(odd), [p for p, _ in pieces], tuple(q for _, q in pieces), [got[s] for s in blocks], blocks, shapes, state["held"]
        )

    def stage(k, *arrived):
        done = [got[s] for s in shares[k - 1]]
        before = state["held"] if k > 1 else send
        arrived, done, before = lax.optimization_barrier((arrived, done, list(before)))
        if k > 1:
            state["held"] = before
        else:
            send[:] = before
            got[0] = send[0]
        for s, v in zip(shares[k - 1], done):
            got[s] = v
            state["blocks"].append(s)
        for s in shares[k]:
            got[s] = chip_swap(send[s], s)
        return arrived

    own = lax.dynamic_slice_in_dim(basis, odd * half, half, 0)
    ids, held = [0], own
    bit, k = chips // 2, 0
    while bit > 1:
        new = chip_swap(held, bit)
        new_ids = [s ^ bit for s in ids]
        k += 1
        held, new = stage(k, held, new)
        state["pieces"].append((new, ("mine", tuple(new_ids))))
        lay()
        held, ids = jnp.concatenate([held, new], 0), ids + new_ids
        bit //= 2
    over_y = chip_swap(held, 1)
    over_x = tile_swap(held[half:])
    over_y, over_x = stage(k + 1, over_y, over_x)
    y_ids, x_ids = [s ^ 1 for s in ids], ids[1:]
    cut = len(ids) // 2
    corner_x = tile_swap(over_y[: cut * half])
    corner_y = chip_swap(over_x[(cut - 1) * half :], 1)
    state["pieces"] += [(over_y, ("mine", tuple(y_ids))), (over_x, ("other", tuple(x_ids)))]
    lay()
    state["pieces"] += [(corner_x, ("other", tuple(y_ids[:cut]))), (corner_y, ("other", tuple(y_ids[cut:])))]
    state["blocks"] += shares[k + 1]
    lay()
    full, x, tails = state["held"]

    inside = (1 - solid).astype(F32)
    ring = jnp.concatenate(
        [
            lax.ppermute(inside[width - HALO :], "tile", [(i, (i + 1) % tiles) for i in range(tiles)]),
            inside,
            lax.ppermute(inside[:HALO], "tile", [((i + 1) % tiles, i) for i in range(tiles)]),
        ]
    )
    e = 2 * z + (y ^ (z % 2))
    g = jnp.where(odd == 0, e, chips - 1 - e)
    fluid = lax.dynamic_slice_in_dim(ring, g * rows, rows + 2 * HALO, 0)
    fluid = jnp.broadcast_to(fluid[:, :, None], fluid.shape + (128,))

    tails = tails.astype(F32)
    values = tails[:, 0:2] + tails[:, 2:4] + tails[:, 4:6]
    want = (core * (chips // 2) + jnp.arange(chips // 2, dtype=jnp.int32)) ^ chip
    pick = want[:, None] == jnp.arange(chips, dtype=jnp.int32)[None, :]
    eigens = jnp.sum(jnp.where(pick[:, :, None, None], values[None], 0.0), axis=1).reshape(1, mine)

    size = mine // CHUNKS
    tile = min(256, size)
    per = size // tile
    halos, solved = [], []
    for j in range(CHUNKS):
        start = i32(((1 - core) * CHUNKS + j) * per, (core * CHUNKS + j) * per)
        if j:
            start, _ = lax.optimization_barrier((start, halos[-1][1]))
        theirs = core_swap(forward(start[:1], x, full, size, tile))
        part = forward(start[1:], x, full, size, tile)
        spectral = (part + theirs).astype(BF16).reshape(rows, wide, size)
        up = lax.ppermute(spectral[rows - HALO :], ("wn", "tile"), onward)
        down = lax.ppermute(spectral[:HALO], ("wn", "tile"), backward)
        halos.append((up, spectral, down))
    others = []
    for j in range(CHUNKS):
        up, spectral, down = halos[j]
        u = sweep(eigens[:, j * size : (j + 1) * size], fluid, up, spectral, down).reshape(cells, size)
        solved.append(u)
        others.append(core_swap(u))

    columns = i32(
        *[core * CHUNKS + j for j in range(CHUNKS)], *[(1 - core) * CHUNKS + j for j in range(CHUNKS)]
    )
    home = [None] * chips
    for i in reversed(range(chips // 2)):
        a, b = inverse(columns, solved + others, full, i, planes)
        columns, a, b = lax.optimization_barrier((columns, a, b))
        home[2 * i + 1] = chip_swap(b, 2 * i + 1)
        home[2 * i] = a if i == 0 else chip_swap(a, 2 * i)

    out = None
    for i in [chips // 2 - 1, *reversed(range(chips // 2 - 2)), chips // 2 - 2]:
        out = place_pair(tables[i], home[2 * i], home[2 * i + 1], out, divergence.shape, rows)
    return out


def solution(mesh):
    return jax.shard_map(
        local,
        mesh=mesh,
        in_specs=(P("wn", "tile", None), P("wn", None), P("wn"), P("wn"), P(), P("tile", None)),
        out_specs=P("wn", "tile", None),
        check_vma=False,
    )
```

```python
import functools
import math

import jax
import jax.numpy as jnp
from jax import lax
from jax.experimental import pallas as pl
from jax.experimental.pallas import tpu as pltpu
from jax.sharding import PartitionSpec as P

SWEEPS = 4
HALO = SWEEPS - 1
CHUNKS = 2
MIB = 1024 * 1024
F32, BF16 = jnp.float32, jnp.bfloat16


def params(mib):
    return pltpu.CompilerParams(vmem_limit_bytes=mib * MIB)


def cost(flops, nbytes):
    return pl.CostEstimate(flops=int(flops), bytes_accessed=int(nbytes), transcendentals=0)


LATE = pl.CostEstimate(flops=40_000_000_000, bytes_accessed=0, transcendentals=0)


def scale_body(table, w_ref, e_ref, x_ref, *o_refs):
    pairs = len(o_refs) // 2
    rows = x_ref.shape[1] // 2
    wide = x_ref.shape[2]
    w = w_ref[...]
    for i in range(pairs):

        @pl.when(pl.program_id(0) == i)
        def _(i=i):
            swap = table[pairs + i] != 0
            a_ref, b_ref = o_refs[2 * i], o_refs[2 * i + 1]
            for r in range(rows):
                low = (x_ref[:, r, :] * w).astype(BF16).T
                high = (x_ref[:, rows + r, :] * w).astype(BF16).T
                a_ref[r * wide : (r + 1) * wide, :] = jnp.where(swap, high, low)
                b_ref[r * wide : (r + 1) * wide, :] = jnp.where(swap, low, high)
            a_ref[rows * wide :, :] = e_ref[...]
            b_ref[rows * wide :, :] = e_ref[...]


def scale(table, weight, extra, divergence, chips):
    planes, width, wide = divergence.shape
    rows, pairs = width // chips, chips // 2
    tall = rows * wide + extra.shape[0]
    return pl.pallas_call(
        scale_body,
        grid_spec=pltpu.PrefetchScalarGridSpec(
            num_scalar_prefetch=1,
            grid=(pairs,),
            in_specs=[
                pl.BlockSpec((planes, 1), lambda i, t: (0, 0)),
                pl.BlockSpec(extra.shape, lambda i, t: (0, 0)),
                pl.BlockSpec((planes, 2 * rows, wide), lambda i, t: (0, t[i], 0)),
            ],
            out_specs=[pl.BlockSpec(memory_space=pltpu.VMEM)] * chips,
        ),
        out_shape=[jax.ShapeDtypeStruct((tall, planes), BF16)] * chips,
        compiler_params=params(12),
        cost_estimate=cost(planes * width * wide, planes * width * wide * 6),
    )(table, weight, extra, divergence)


def place_body(table, *refs):
    a_ref, b_ref, o_ref = refs[0], refs[1], refs[-1]
    rows = o_ref.shape[1] // 2
    wide = o_ref.shape[2]
    swap = table[1] != 0
    for r in range(rows):
        a = a_ref[r * wide : (r + 1) * wide, :]
        b = b_ref[r * wide : (r + 1) * wide, :]
        o_ref[:, r, :] = jnp.where(swap, b, a).T.astype(F32)
        o_ref[:, rows + r, :] = jnp.where(swap, a, b).T.astype(F32)


def place_pair(table, a, b, out, shape, rows):
    planes, _, wide = shape
    spec = pl.BlockSpec((rows * wide, planes), lambda i, t: (0, 0))
    ins, specs, alias = [a, b], [spec, spec], {}
    if out is not None:
        ins.append(out)
        specs.append(pl.BlockSpec(memory_space=pl.ANY))
        alias = {3: 0}
    return pl.pallas_call(
        place_body,
        grid_spec=pltpu.PrefetchScalarGridSpec(
            num_scalar_prefetch=1,
            grid=(1,),
            in_specs=specs,
            out_specs=pl.BlockSpec((planes, 2 * rows, wide), lambda i, t: (0, t[0], 0)),
        ),
        out_shape=jax.ShapeDtypeStruct(shape, F32),
        input_output_aliases=alias,
        compiler_params=params(12),
        cost_estimate=cost(planes * rows * wide * 2, planes * rows * wide * 12),
    )(table, *ins)


def run_copies(copies, sem):
    handles = [pltpu.make_async_copy(p, q, sem.at[k]) for k, (p, q) in enumerate(copies)]
    for h in handles:
        h.start()
    for h in handles:
        h.wait()


def gather_body(blocks, *refs):
    x_refs, (o_ref, e_ref, sem) = refs[: len(blocks)], refs[-3:]
    cells, planes = o_ref.shape[-2], x_refs[0].shape[1]
    copies = []
    for ref, s in zip(x_refs, blocks):
        tail = ref.shape[0] - cells
        copies.append((ref.at[pl.ds(cells, tail), :], e_ref.at[s]))
        place = o_ref.at[s] if len(o_ref.shape) == 3 else o_ref.at[:, pl.ds(s * planes, planes)]
        copies.append((ref.at[pl.ds(0, cells), :], place))
    run_copies(copies, sem)


def gather(xs, blocks, cells, chips, held, mark):
    tall, planes = xs[0].shape
    out = [
        pltpu.VMEM((chips, cells, planes) if planes % 128 else (cells, chips * planes), BF16),
        pltpu.VMEM((chips, tall - cells, planes), BF16),
    ]
    count = len(xs) + (len(held) if held else 0)
    return pl.pallas_call(
        functools.partial(gather_body, tuple(blocks)),
        in_specs=[pl.BlockSpec(memory_space=pltpu.VMEM)] * count,
        out_specs=[pl.BlockSpec(memory_space=pltpu.VMEM)] * 2,
        out_shape=out,
        input_output_aliases={len(xs): 0, len(xs) + 1: 1} if held else {},
        scratch_shapes=[pltpu.SemaphoreType.DMA((2 * len(xs),))],
        compiler_params=params(12),
        cost_estimate=mark,
    )(*xs, *(held or []))


def join_body(layout, planes, half_ref, *refs):
    b_refs, (out, sem) = refs[: len(layout)], refs[-2:]
    part = planes // 2
    half = half_ref[0]
    copies = []
    for ref, (kind, ids) in zip(b_refs, layout):
        for j, s in enumerate(ids):
            if kind == "whole":
                src, dst = ref, out.at[pl.ds(s * planes, planes), :]
            else:
                side = half if kind == "mine" else 1 - half
                start = pl.multiple_of(s * planes + side * part, part)
                src, dst = ref.at[pl.ds(j * part, part), :], out.at[pl.ds(start, part), :]
            copies.append((src, dst))
    run_copies(copies, sem)


def join(half, pieces, layout, planes, chips, held, mark):
    modes = pieces[0].shape[1]
    home = pl.BlockSpec(memory_space=pltpu.HBM)
    specs = [pl.BlockSpec(memory_space=pltpu.SMEM)] + [pl.BlockSpec(memory_space=pltpu.VMEM)] * len(pieces)
    ins, alias = list(pieces), {}
    if held is not None:
        alias = {1 + len(ins): 0}
        specs.append(home)
        ins.append(held)
    return pl.pallas_call(
        functools.partial(join_body, layout, planes),
        in_specs=specs,
        out_specs=home,
        out_shape=pltpu.HBM((chips * planes, modes), BF16),
        input_output_aliases=alias,
        scratch_shapes=[pltpu.SemaphoreType.DMA((sum(len(ids) for _, ids in layout),))],
        compiler_params=params(12),
        cost_estimate=mark,
    )(half, *ins)


def forward_body(table, x_ref, b_ref, *refs):
    x = x_ref[...]
    if len(x.shape) == 3:
        x = jnp.concatenate([x[k] for k in range(x.shape[0])], axis=1)
    total = jnp.dot(x, b_ref[...], preferred_element_type=F32)
    if len(refs) == 2:
        total = total + refs[0][...]
    refs[-1][...] = total.astype(refs[-1].dtype)


def forward(table, x, basis, modes, tile, theirs=None):
    cells, depth = x.shape[-2], basis.shape[0]
    extra = [] if theirs is None else [theirs]
    return pl.pallas_call(
        forward_body,
        grid_spec=pltpu.PrefetchScalarGridSpec(
            num_scalar_prefetch=1,
            grid=(modes // tile,),
            in_specs=[
                pl.BlockSpec(memory_space=pltpu.VMEM),
                pl.BlockSpec((depth, tile), lambda j, t: (0, t[0] + j)),
            ]
            + [pl.BlockSpec((cells, tile), lambda j, t: (0, j))] * len(extra),
            out_specs=pl.BlockSpec((cells, tile), lambda j, t: (0, j)),
        ),
        out_shape=jax.ShapeDtypeStruct((cells, modes), BF16 if extra else F32),
        compiler_params=params(16),
        cost_estimate=cost(2 * cells * depth * modes, 2 * cells * depth + 2 * depth * modes + 4 * cells * modes),
    )(table, x, basis, *extra)


def sweep_body(eigen_ref, fluid_ref, up_ref, own_ref, down_ref, o_ref, rhs, ua, ub):
    rows = own_ref.shape[0]
    ext = rows + 2 * HALO
    diag = eigen_ref[...] + 4.0
    spread = 4.0 / diag
    keep, gain = [], []
    for step in range(SWEEPS):
        omega = 1.0 / (1.0 + spread * math.cos(math.pi * (2 * step + 1) / (2 * SWEEPS)))
        keep.append(1.0 - omega)
        gain.append(omega / diag)

    def load(ref, first):
        def body(r, _):
            s = ref[r].astype(F32)
            rhs[first + r] = s
            ua[first + r] = fluid_ref[first + r] * (gain[0] * s)
            return 0

        lax.fori_loop(0, ref.shape[0], body, 0)

    load(up_ref, 0)
    load(own_ref, HALO)
    load(down_ref, HALO + rows)
    src, dst = ua, ub
    for step in range(1, SWEEPS):
        last = step == SWEEPS - 1

        def body(r, _, src=src, dst=dst, step=step, last=last):
            c = src[r]
            wide = c.shape[0]
            beside = src[r - 1] + src[r + 1] + (pltpu.roll(c, 1, 0) + pltpu.roll(c, wide - 1, 0))
            new = fluid_ref[r] * (keep[step] * c + gain[step] * (rhs[r] + beside))
            if last:
                o_ref[r - HALO] = new.astype(BF16)
            else:
                dst[r] = new
            return 0

        lax.fori_loop(step, ext - step, body, 0)
        src, dst = dst, src


def sweep(eigen, fluid, up, own, down):
    rows, wide, modes = own.shape
    ext, lanes = rows + 2 * HALO, 128
    block = lambda n: pl.BlockSpec((n, wide, lanes), lambda j: (0, 0, j))
    return pl.pallas_call(
        sweep_body,
        grid=(modes // lanes,),
        in_specs=[
            pl.BlockSpec((1, lanes), lambda j: (0, j)),
            pl.BlockSpec((ext, wide, lanes), lambda j: (0, 0, 0)),
            block(HALO),
            block(rows),
            block(HALO),
        ],
        out_specs=block(rows),
        out_shape=jax.ShapeDtypeStruct((rows, wide, modes), BF16),
        scratch_shapes=[pltpu.VMEM((ext, wide, lanes), F32)] * 3,
        compiler_params=params(16),
        cost_estimate=cost(modes * wide * ext * 400, 4 * modes * wide * ext),
    )(eigen, fluid, up, own, down)


def inverse_body(tile, table, *refs):
    parts, b_ref, o_refs = refs[:-3], refs[-3], refs[-2:]
    cells, wide = parts[0].shape
    planes = o_refs[0].shape[1]

    def body(i, _):
        rows = pl.ds(pl.multiple_of(i * tile, tile), tile)
        total = None
        for k, part in enumerate(parts):
            cols = pl.ds(pl.multiple_of(table[k] * wide, wide), wide)
            term = lax.dot_general(
                part[rows, :], b_ref[:, cols], (((1,), (1,)), ((), ())), preferred_element_type=F32
            )
            total = term if total is None else total + term
        o_refs[0][rows, :] = total[:, :planes].astype(BF16)
        o_refs[1][rows, :] = total[:, planes:].astype(BF16)
        return 0

    lax.fori_loop(0, cells // tile, body, 0)


def inverse(table, parts, basis, pair, planes):
    cells, wide = parts[0].shape
    modes = basis.shape[1]
    out = jax.ShapeDtypeStruct((cells, planes), BF16)
    whole = pl.BlockSpec(memory_space=pltpu.VMEM)
    return pl.pallas_call(
        functools.partial(inverse_body, min(cells, 256)),
        grid=(1,),
        in_specs=[pl.BlockSpec(memory_space=pltpu.SMEM)]
        + [whole] * len(parts)
        + [pl.BlockSpec((2 * planes, modes), lambda i: (pair, 0))],
        out_specs=[whole] * 2,
        out_shape=[out, out],
        compiler_params=params(16),
        cost_estimate=cost(4 * cells * modes * planes, 2 * cells * modes + 4 * planes * modes),
    )(table, *parts, basis)


def local(divergence, basis, eigen, plane_level, spacing, solid):
    planes, width, wide = divergence.shape
    wn, tiles = lax.axis_size("wn"), lax.axis_size("tile")
    chips = wn // 2
    rows = width // chips
    cells = rows * wide
    modes = basis.shape[1]
    mine = modes // 2
    me, t = lax.axis_index("wn"), lax.axis_index("tile")
    core, chip = me % 2, me // 2
    z, y, odd = chip // 2, chip % 2, t % 2
    i32 = lambda *v: jnp.stack([jnp.asarray(x, jnp.int32) for x in v])

    flip = lambda s: [(i, i ^ (2 * s)) for i in range(wn)]
    chip_swap = lambda v, s: lax.ppermute(v, "wn", flip(s))
    core_swap = lambda v: lax.ppermute(v, "wn", [(i, i ^ 1) for i in range(wn)])
    tile_swap = lambda v: lax.ppermute(v, "tile", [(i, i ^ 1) for i in range(tiles)])

    def pair_table(i):
        pz = z ^ i
        block = jnp.where(odd == 0, pz, chips // 2 - 1 - pz)
        return i32(block, y ^ (pz % 2) ^ odd)

    tables = [pair_table(i) for i in range(chips // 2)]
    order = lambda g: (g // 2) * 2 + ((g % 2) ^ ((g // 2) % 2))

    def device(tt, g):
        return order(g if tt % 2 == 0 else chips - 1 - g)

    snake = [(tt, device(tt, g)) for tt in range(tiles) for g in range(chips)]
    onward = [
        ((qa * 2 + c) * tiles + ta, (qb * 2 + c) * tiles + tb)
        for (ta, qa), (tb, qb) in zip(snake, snake[1:] + snake[:1])
        for c in range(2)
    ]
    backward = [(b, a) for a, b in onward]

    onehot = (plane_level[:, None] == jnp.arange(spacing.shape[0], dtype=jnp.int32)[None, :]).astype(F32)
    weight = jnp.sum(onehot * spacing[None, :], axis=1)[:, None]

    sibling = core_swap(eigen)
    both = jnp.stack([jnp.where(core == 0, eigen, sibling), jnp.where(core == 0, sibling, eigen)])
    high = lax.reduce_precision(both, 8, 7)
    middle = lax.reduce_precision(both - high, 8, 7)
    low = both - high - middle
    extra = jnp.concatenate([high, middle, low, jnp.zeros((10, planes), F32)]).astype(BF16)

    inside = (1 - solid).astype(F32)
    edges = [
        lax.ppermute(inside[width - HALO :], "tile", [(i, (i + 1) % tiles) for i in range(tiles)]),
        lax.ppermute(inside[:HALO], "tile", [((i + 1) % tiles, i) for i in range(tiles)]),
    ]

    divergence = pltpu.with_memory_space_constraint(divergence, pltpu.HBM)
    extra, edges = lax.optimization_barrier((extra, edges))
    blocks = [table[0] for table in tables] + [table[1] for table in tables]
    send = scale(i32(*blocks), weight, extra, divergence, chips)

    half = planes // 2
    far = chips // 2
    ids = tuple(range(2, chips, 2))
    odds = tuple(range(1, chips, 2))
    small = cost(0, 1 << 20)

    own = lax.dynamic_slice_in_dim(basis, odd * half, half, 0)
    column = [chip_swap(own, s) for s in ids]
    beside = chip_swap(own, 1)
    layout = (("whole", (0,)), *[("mine", (s,)) for s in ids], ("mine", (1,)))
    full = join(i32(odd), [basis, *column, beside], layout, planes, chips, None, LATE)
    column, beside, full, send = lax.optimization_barrier((column, beside, full, send))

    held = jnp.concatenate(column)
    over_y, over_x = chip_swap(held, 1), tile_swap(jnp.concatenate([held, beside]))
    evens = list(range(far, chips, 2))
    x = gather([send[0], *[chip_swap(send[s], s) for s in evens]], [0, *evens], cells, chips, None, LATE)
    over_y, over_x, x, send = lax.optimization_barrier((over_y, over_x, x, send))

    corner = tile_swap(over_y)
    full = join(i32(odd), [over_y, over_x], (("mine", odds[1:]), ("other", (*ids, 1))), planes, chips, full, small)
    last = list(range(far + 1, chips, 2))
    x = gather([chip_swap(send[s], s) for s in last], last, cells, chips, x, LATE)
    nearby = list(range(1, far))
    x = gather([chip_swap(send[s], s) for s in nearby], nearby, cells, chips, x, small)
    full, x, corner = lax.optimization_barrier((full, x, corner))
    full = join(i32(odd), [corner], (("other", odds[1:]),), planes, chips, full, small)
    x, tails = x

    ring = jnp.concatenate([edges[0], inside, edges[1]])
    e = 2 * z + (y ^ (z % 2))
    g = jnp.where(odd == 0, e, chips - 1 - e)
    fluid = lax.dynamic_slice_in_dim(ring, g * rows, rows + 2 * HALO, 0)
    fluid = jnp.broadcast_to(fluid[:, :, None], fluid.shape + (128,))

    tails = tails.astype(F32)
    values = tails[:, 0:2] + tails[:, 2:4] + tails[:, 4:6]
    want = (core * (chips // 2) + jnp.arange(chips // 2, dtype=jnp.int32)) ^ chip
    pick = want[:, None] == jnp.arange(chips, dtype=jnp.int32)[None, :]
    eigens = jnp.sum(jnp.where(pick[:, :, None, None], values[None], 0.0), axis=1).reshape(1, mine)

    size = mine // CHUNKS
    tile = min(256, size)
    per = size // tile
    stored = pltpu.with_memory_space_constraint(full, pltpu.HBM)
    halos, solved, theirs = [], [], []
    mark = None
    for j in range(CHUNKS):
        start = i32(((1 - core) * CHUNKS + j) * per)
        if mark is not None:
            start, mark = lax.optimization_barrier((start, mark))
        mark = forward(start, x, stored, size, tile)
        theirs.append(core_swap(mark))
    for j in range(CHUNKS):
        start = i32((core * CHUNKS + j) * per)
        start, mark = lax.optimization_barrier((start, mark))
        mark = forward(start, x, stored, size, tile, theirs[j])
        spectral = mark.reshape(rows, wide, size)
        up = lax.ppermute(spectral[rows - HALO :], ("wn", "tile"), onward)
        down = lax.ppermute(spectral[:HALO], ("wn", "tile"), backward)
        halos.append((up, spectral, down))
    others = []
    for j in range(CHUNKS):
        up, spectral, down = halos[j]
        u = sweep(eigens[:, j * size : (j + 1) * size], fluid, up, spectral, down).reshape(cells, size)
        solved.append(u)
        others.append(core_swap(u))

    columns = i32(
        *[core * CHUNKS + j for j in range(CHUNKS)], *[(1 - core) * CHUNKS + j for j in range(CHUNKS)]
    )
    home = [None] * chips
    pairs = list(range(chips // 2))
    for i in [0, *reversed(pairs[1:])]:
        home[2 * i], home[2 * i + 1] = inverse(columns, solved + others, full, i, planes)
    first = [1, *[s for i in reversed(pairs[chips // 4 + 1 :]) for s in (2 * i + 1, 2 * i)]]
    second = [s for i in reversed(pairs[1 : chips // 4 + 1]) for s in (2 * i + 1, 2 * i)]
    held = [home[s] for s in second]
    for s in first:
        home[s] = chip_swap(home[s], s)
    home[1], held = lax.optimization_barrier((home[1], held))
    for s, v in zip(second, held):
        home[s] = chip_swap(v, s)

    out = None
    for i in [0, *pairs[chips // 4 + 1 :], *pairs[1 : chips // 4 + 1]]:
        out = place_pair(tables[i], home[2 * i], home[2 * i + 1], out, divergence.shape, rows)
    return out


def solution(mesh):
    return jax.shard_map(
        local,
        mesh=mesh,
        in_specs=(P("wn", "tile", None), P("wn", None), P("wn"), P("wn"), P(), P("tile", None)),
        out_specs=P("wn", "tile", None),
        check_vma=False,
    )
```

```python
import functools
import math

import jax
import jax.numpy as jnp
from jax import lax
from jax.experimental import pallas as pl
from jax.experimental.pallas import tpu as pltpu
from jax.sharding import PartitionSpec as P

SWEEPS = 4
HALO = SWEEPS - 1
CHUNKS = 2
MIB = 1024 * 1024
F32, BF16 = jnp.float32, jnp.bfloat16


def params(mib):
    return pltpu.CompilerParams(vmem_limit_bytes=mib * MIB)


def cost(flops, nbytes):
    return pl.CostEstimate(flops=int(flops), bytes_accessed=int(nbytes), transcendentals=0)


LATE = pl.CostEstimate(flops=40_000_000_000, bytes_accessed=0, transcendentals=0)


def scale_body(table, w_ref, e_ref, x_ref, *o_refs):
    pairs = len(o_refs) // 2
    rows = x_ref.shape[1] // 2
    wide = x_ref.shape[2]
    w = w_ref[...]
    for i in range(pairs):

        @pl.when(pl.program_id(0) == i)
        def _(i=i):
            swap = table[pairs + i] != 0
            a_ref, b_ref = o_refs[2 * i], o_refs[2 * i + 1]
            for r in range(rows):
                low = (x_ref[:, r, :] * w).astype(BF16).T
                high = (x_ref[:, rows + r, :] * w).astype(BF16).T
                a_ref[r * wide : (r + 1) * wide, :] = jnp.where(swap, high, low)
                b_ref[r * wide : (r + 1) * wide, :] = jnp.where(swap, low, high)
            a_ref[rows * wide :, :] = e_ref[...]
            b_ref[rows * wide :, :] = e_ref[...]


def scale(table, weight, extra, divergence, chips):
    planes, width, wide = divergence.shape
    rows, pairs = width // chips, chips // 2
    tall = rows * wide + extra.shape[0]
    return pl.pallas_call(
        scale_body,
        grid_spec=pltpu.PrefetchScalarGridSpec(
            num_scalar_prefetch=1,
            grid=(pairs,),
            in_specs=[
                pl.BlockSpec((planes, 1), lambda i, t: (0, 0)),
                pl.BlockSpec(extra.shape, lambda i, t: (0, 0)),
                pl.BlockSpec((planes, 2 * rows, wide), lambda i, t: (0, t[i], 0)),
            ],
            out_specs=[pl.BlockSpec(memory_space=pltpu.VMEM)] * chips,
        ),
        out_shape=[jax.ShapeDtypeStruct((tall, planes), BF16)] * chips,
        compiler_params=params(12),
        cost_estimate=cost(planes * width * wide, planes * width * wide * 6),
    )(table, weight, extra, divergence)


def place_body(table, *refs):
    a_ref, b_ref, o_ref = refs[0], refs[1], refs[-1]
    rows = o_ref.shape[1] // 2
    wide = o_ref.shape[2]
    swap = table[1] != 0
    for r in range(rows):
        a = a_ref[r * wide : (r + 1) * wide, :]
        b = b_ref[r * wide : (r + 1) * wide, :]
        o_ref[:, r, :] = jnp.where(swap, b, a).T.astype(F32)
        o_ref[:, rows + r, :] = jnp.where(swap, a, b).T.astype(F32)


def place_pair(table, a, b, out, shape, rows):
    planes, _, wide = shape
    spec = pl.BlockSpec((rows * wide, planes), lambda i, t: (0, 0))
    ins, specs, alias = [a, b], [spec, spec], {}
    if out is not None:
        ins.append(out)
        specs.append(pl.BlockSpec(memory_space=pl.ANY))
        alias = {3: 0}
    return pl.pallas_call(
        place_body,
        grid_spec=pltpu.PrefetchScalarGridSpec(
            num_scalar_prefetch=1,
            grid=(1,),
            in_specs=specs,
            out_specs=pl.BlockSpec((planes, 2 * rows, wide), lambda i, t: (0, t[0], 0)),
        ),
        out_shape=jax.ShapeDtypeStruct(shape, F32),
        input_output_aliases=alias,
        compiler_params=params(12),
        cost_estimate=cost(planes * rows * wide * 2, planes * rows * wide * 12),
    )(table, *ins)


def run_copies(copies, sem):
    handles = [pltpu.make_async_copy(p, q, sem.at[k]) for k, (p, q) in enumerate(copies)]
    for h in handles:
        h.start()
    for h in handles:
        h.wait()


def gather_body(blocks, *refs):
    x_refs, (o_ref, e_ref, sem) = refs[: len(blocks)], refs[-3:]
    cells, planes = o_ref.shape[-2], x_refs[0].shape[1]
    copies = []
    for ref, s in zip(x_refs, blocks):
        tail = ref.shape[0] - cells
        copies.append((ref.at[pl.ds(cells, tail), :], e_ref.at[s]))
        place = o_ref.at[s] if len(o_ref.shape) == 3 else o_ref.at[:, pl.ds(s * planes, planes)]
        copies.append((ref.at[pl.ds(0, cells), :], place))
    run_copies(copies, sem)


def gather(xs, blocks, cells, chips, held, mark):
    tall, planes = xs[0].shape
    out = [
        pltpu.VMEM((chips, cells, planes) if planes % 128 else (cells, chips * planes), BF16),
        pltpu.VMEM((chips, tall - cells, planes), BF16),
    ]
    count = len(xs) + (len(held) if held else 0)
    return pl.pallas_call(
        functools.partial(gather_body, tuple(blocks)),
        in_specs=[pl.BlockSpec(memory_space=pltpu.VMEM)] * count,
        out_specs=[pl.BlockSpec(memory_space=pltpu.VMEM)] * 2,
        out_shape=out,
        input_output_aliases={len(xs): 0, len(xs) + 1: 1} if held else {},
        scratch_shapes=[pltpu.SemaphoreType.DMA((2 * len(xs),))],
        compiler_params=params(12),
        cost_estimate=mark,
    )(*xs, *(held or []))


def join_body(layout, planes, half_ref, *refs):
    b_refs, (out, sem) = refs[: len(layout)], refs[-2:]
    part = planes // 2
    half = half_ref[0]
    copies = []
    for ref, (kind, ids) in zip(b_refs, layout):
        for j, s in enumerate(ids):
            if kind == "whole":
                src, dst = ref, out.at[pl.ds(s * planes, planes), :]
            else:
                side = half if kind == "mine" else 1 - half
                start = pl.multiple_of(s * planes + side * part, part)
                src, dst = ref.at[pl.ds(j * part, part), :], out.at[pl.ds(start, part), :]
            copies.append((src, dst))
    run_copies(copies, sem)


def join(half, pieces, layout, planes, chips, held, mark):
    modes = pieces[0].shape[1]
    home = pl.BlockSpec(memory_space=pltpu.HBM)
    specs = [pl.BlockSpec(memory_space=pltpu.SMEM)] + [pl.BlockSpec(memory_space=pltpu.VMEM)] * len(pieces)
    ins, alias = list(pieces), {}
    if held is not None:
        alias = {1 + len(ins): 0}
        specs.append(home)
        ins.append(held)
    return pl.pallas_call(
        functools.partial(join_body, layout, planes),
        in_specs=specs,
        out_specs=home,
        out_shape=pltpu.HBM((chips * planes, modes), BF16),
        input_output_aliases=alias,
        scratch_shapes=[pltpu.SemaphoreType.DMA((sum(len(ids) for _, ids in layout),))],
        compiler_params=params(12),
        cost_estimate=mark,
    )(half, *ins)


def forward_body(table, x_ref, b_ref, *refs):
    x = x_ref[...]
    if len(x.shape) == 3:
        x = jnp.concatenate([x[k] for k in range(x.shape[0])], axis=1)
    total = jnp.dot(x, b_ref[...], preferred_element_type=F32)
    if len(refs) == 2:
        total = total + refs[0][...]
    refs[-1][...] = total.astype(refs[-1].dtype)


def forward(table, x, basis, modes, tile, theirs=None):
    cells, depth = x.shape[-2], basis.shape[0]
    extra = [] if theirs is None else [theirs]
    return pl.pallas_call(
        forward_body,
        grid_spec=pltpu.PrefetchScalarGridSpec(
            num_scalar_prefetch=1,
            grid=(modes // tile,),
            in_specs=[
                pl.BlockSpec(memory_space=pltpu.VMEM),
                pl.BlockSpec((depth, tile), lambda j, t: (0, t[0] + j)),
            ]
            + [pl.BlockSpec((cells, tile), lambda j, t: (0, j))] * len(extra),
            out_specs=pl.BlockSpec((cells, tile), lambda j, t: (0, j)),
        ),
        out_shape=jax.ShapeDtypeStruct((cells, modes), BF16 if extra else F32),
        compiler_params=params(16),
        cost_estimate=cost(2 * cells * depth * modes, 2 * cells * depth + 2 * depth * modes + 4 * cells * modes),
    )(table, x, basis, *extra)


def sweep_body(eigen_ref, fluid_ref, up_ref, own_ref, down_ref, o_ref, rhs, ua, ub):
    rows = own_ref.shape[0]
    ext = rows + 2 * HALO
    diag = eigen_ref[...] + 4.0
    spread = 4.0 / diag
    keep, gain = [], []
    for step in range(SWEEPS):
        omega = 1.0 / (1.0 + spread * math.cos(math.pi * (2 * step + 1) / (2 * SWEEPS)))
        keep.append(1.0 - omega)
        gain.append(omega / diag)

    for ref, first in ((up_ref, 0), (own_ref, HALO), (down_ref, HALO + rows)):
        for r in range(ref.shape[0]):
            s = ref[r].astype(F32)
            rhs[first + r] = s
            ua[first + r] = fluid_ref[first + r] * (gain[0] * s)
    src, dst = ua, ub
    for step in range(1, SWEEPS):
        for r in range(step, ext - step):
            c = src[r]
            wide = c.shape[0]
            beside = src[r - 1] + src[r + 1] + (pltpu.roll(c, 1, 0) + pltpu.roll(c, wide - 1, 0))
            new = fluid_ref[r] * (keep[step] * c + gain[step] * (rhs[r] + beside))
            if step == SWEEPS - 1:
                o_ref[r - HALO] = new.astype(BF16)
            else:
                dst[r] = new
        src, dst = dst, src


def sweep(eigen, fluid, up, own, down):
    rows, wide, modes = own.shape
    ext, lanes = rows + 2 * HALO, 128
    block = lambda n: pl.BlockSpec((n, wide, lanes), lambda j: (0, 0, j))
    return pl.pallas_call(
        sweep_body,
        grid=(modes // lanes,),
        in_specs=[
            pl.BlockSpec((1, lanes), lambda j: (0, j)),
            pl.BlockSpec((ext, wide, lanes), lambda j: (0, 0, 0)),
            block(HALO),
            block(rows),
            block(HALO),
        ],
        out_specs=block(rows),
        out_shape=jax.ShapeDtypeStruct((rows, wide, modes), BF16),
        scratch_shapes=[pltpu.VMEM((ext, wide, lanes), F32)] * 3,
        compiler_params=params(16),
        cost_estimate=cost(modes * wide * ext * 400, 4 * modes * wide * ext),
    )(eigen, fluid, up, own, down)


def inverse_body(tile, table, *refs):
    parts, b_ref, o_refs = refs[:-3], refs[-3], refs[-2:]
    cells, wide = parts[0].shape
    planes = o_refs[0].shape[1]

    def body(i, _):
        rows = pl.ds(pl.multiple_of(i * tile, tile), tile)
        total = None
        for k, part in enumerate(parts):
            cols = pl.ds(pl.multiple_of(table[k] * wide, wide), wide)
            term = lax.dot_general(
                part[rows, :], b_ref[:, cols], (((1,), (1,)), ((), ())), preferred_element_type=F32
            )
            total = term if total is None else total + term
        o_refs[0][rows, :] = total[:, :planes].astype(BF16)
        o_refs[1][rows, :] = total[:, planes:].astype(BF16)
        return 0

    lax.fori_loop(0, cells // tile, body, 0)


def inverse(table, parts, basis, pair, planes):
    cells, wide = parts[0].shape
    modes = basis.shape[1]
    out = jax.ShapeDtypeStruct((cells, planes), BF16)
    whole = pl.BlockSpec(memory_space=pltpu.VMEM)
    return pl.pallas_call(
        functools.partial(inverse_body, min(cells, 256)),
        grid=(1,),
        in_specs=[pl.BlockSpec(memory_space=pltpu.SMEM)]
        + [whole] * len(parts)
        + [pl.BlockSpec((2 * planes, modes), lambda i: (pair, 0))],
        out_specs=[whole] * 2,
        out_shape=[out, out],
        compiler_params=params(16),
        cost_estimate=cost(4 * cells * modes * planes, 2 * cells * modes + 4 * planes * modes),
    )(table, *parts, basis)


def local(divergence, basis, eigen, plane_level, spacing, solid):
    planes, width, wide = divergence.shape
    wn, tiles = lax.axis_size("wn"), lax.axis_size("tile")
    chips = wn // 2
    rows = width // chips
    cells = rows * wide
    modes = basis.shape[1]
    mine = modes // 2
    me, t = lax.axis_index("wn"), lax.axis_index("tile")
    core, chip = me % 2, me // 2
    z, y, odd = chip // 2, chip % 2, t % 2
    i32 = lambda *v: jnp.stack([jnp.asarray(x, jnp.int32) for x in v])

    flip = lambda s: [(i, i ^ (2 * s)) for i in range(wn)]
    chip_swap = lambda v, s: lax.ppermute(v, "wn", flip(s))
    core_swap = lambda v: lax.ppermute(v, "wn", [(i, i ^ 1) for i in range(wn)])
    tile_swap = lambda v: lax.ppermute(v, "tile", [(i, i ^ 1) for i in range(tiles)])

    def pair_table(i):
        pz = z ^ i
        block = jnp.where(odd == 0, pz, chips // 2 - 1 - pz)
        return i32(block, y ^ (pz % 2) ^ odd)

    tables = [pair_table(i) for i in range(chips // 2)]
    order = lambda g: (g // 2) * 2 + ((g % 2) ^ ((g // 2) % 2))

    def device(tt, g):
        return order(g if tt % 2 == 0 else chips - 1 - g)

    snake = [(tt, device(tt, g)) for tt in range(tiles) for g in range(chips)]
    onward = [
        ((qa * 2 + c) * tiles + ta, (qb * 2 + c) * tiles + tb)
        for (ta, qa), (tb, qb) in zip(snake, snake[1:] + snake[:1])
        for c in range(2)
    ]
    backward = [(b, a) for a, b in onward]

    onehot = (plane_level[:, None] == jnp.arange(spacing.shape[0], dtype=jnp.int32)[None, :]).astype(F32)
    weight = jnp.sum(onehot * spacing[None, :], axis=1)[:, None]

    sibling = core_swap(eigen)
    both = jnp.stack([jnp.where(core == 0, eigen, sibling), jnp.where(core == 0, sibling, eigen)])
    high = lax.reduce_precision(both, 8, 7)
    middle = lax.reduce_precision(both - high, 8, 7)
    low = both - high - middle
    extra = jnp.concatenate([high, middle, low, jnp.zeros((10, planes), F32)]).astype(BF16)

    inside = (1 - solid).astype(F32)
    edges = [
        lax.ppermute(inside[width - HALO :], "tile", [(i, (i + 1) % tiles) for i in range(tiles)]),
        lax.ppermute(inside[:HALO], "tile", [((i + 1) % tiles, i) for i in range(tiles)]),
    ]

    divergence = pltpu.with_memory_space_constraint(divergence, pltpu.HBM)
    extra, edges = lax.optimization_barrier((extra, edges))
    blocks = [table[0] for table in tables] + [table[1] for table in tables]
    send = scale(i32(*blocks), weight, extra, divergence, chips)

    half = planes // 2
    far = chips // 2
    ids = tuple(range(2, chips, 2))
    odds = tuple(range(1, chips, 2))
    small = cost(0, 1 << 20)

    own = lax.dynamic_slice_in_dim(basis, odd * half, half, 0)
    column = [chip_swap(own, s) for s in ids]
    beside = chip_swap(basis, 1)
    layout = (("whole", (0,)), *[("mine", (s,)) for s in ids], ("whole", (1,)))
    full = join(i32(odd), [basis, *column, beside], layout, planes, chips, None, LATE)
    column, beside, full, send = lax.optimization_barrier((column, beside, full, send))

    held = jnp.concatenate(column)
    over_y, over_x = chip_swap(held, 1), tile_swap(held)
    evens = list(range(far, far + far // 2))
    x = gather([send[0], *[chip_swap(send[s], s) for s in evens]], [0, *evens], cells, chips, None, LATE)
    over_y, over_x, x, send = lax.optimization_barrier((over_y, over_x, x, send))

    cut = (2 * len(ids) + 2) // 3
    corner_x, corner_y = tile_swap(over_y[: cut * half]), chip_swap(over_x[cut * half :], 1)
    full = join(i32(odd), [over_y, over_x], (("mine", odds[1:]), ("other", ids)), planes, chips, full, small)
    last, nearby = list(range(far + far // 2, chips)), list(range(1, far))
    final = [chip_swap(send[s], s) for s in last]
    x = gather([chip_swap(send[s], s) for s in nearby], nearby, cells, chips, x, small)
    corner_x, corner_y, x = lax.optimization_barrier((corner_x, corner_y, x))
    x = gather(final, last, cells, chips, x, LATE)
    layout = (("other", odds[1 : cut + 1]), ("other", odds[cut + 1 :]))
    full = join(i32(odd), [corner_x, corner_y], layout, planes, chips, full, small)
    x, tails = x

    ring = jnp.concatenate([edges[0], inside, edges[1]])
    e = 2 * z + (y ^ (z % 2))
    g = jnp.where(odd == 0, e, chips - 1 - e)
    fluid = lax.dynamic_slice_in_dim(ring, g * rows, rows + 2 * HALO, 0)
    fluid = jnp.broadcast_to(fluid[:, :, None], fluid.shape + (128,))

    tails = tails.astype(F32)
    values = tails[:, 0:2] + tails[:, 2:4] + tails[:, 4:6]
    want = (core * (chips // 2) + jnp.arange(chips // 2, dtype=jnp.int32)) ^ chip
    pick = want[:, None] == jnp.arange(chips, dtype=jnp.int32)[None, :]
    eigens = jnp.sum(jnp.where(pick[:, :, None, None], values[None], 0.0), axis=1).reshape(1, mine)

    size = mine // CHUNKS
    tile = min(256, size)
    per = size // tile
    stored = pltpu.with_memory_space_constraint(full, pltpu.HBM)
    halos, solved, theirs = [], [], []
    mark = None
    for j in range(CHUNKS):
        start = i32(((1 - core) * CHUNKS + j) * per)
        if mark is not None:
            start, mark = lax.optimization_barrier((start, mark))
        mark = forward(start, x, stored, size, tile)
        theirs.append(core_swap(mark))
    for j in range(CHUNKS):
        start = i32((core * CHUNKS + j) * per)
        start, mark = lax.optimization_barrier((start, mark))
        mark = forward(start, x, stored, size, tile, theirs[j])
        spectral = mark.reshape(rows, wide, size)
        up = lax.ppermute(spectral[rows - HALO :], ("wn", "tile"), onward)
        down = lax.ppermute(spectral[:HALO], ("wn", "tile"), backward)
        halos.append((up, spectral, down))
    others = []
    for j in range(CHUNKS):
        up, spectral, down = halos[j]
        u = sweep(eigens[:, j * size : (j + 1) * size], fluid, up, spectral, down).reshape(cells, size)
        solved.append(u)
        others.append(core_swap(u))

    columns = i32(
        *[core * CHUNKS + j for j in range(CHUNKS)], *[(1 - core) * CHUNKS + j for j in range(CHUNKS)]
    )
    home = [None] * chips
    pairs = list(range(chips // 2))
    for i in reversed(pairs):
        home[2 * i], home[2 * i + 1] = inverse(columns, solved + others, full, i, planes)
    first = [s for i in reversed(pairs[chips // 4 + 1 :]) for s in (2 * i + 1, 2 * i)]
    second = [s for i in reversed(pairs[: chips // 4 + 1]) for s in (2 * i + 1, 2 * i) if s]
    held = [home[s] for s in second]
    sign = core_swap(home[first[0]][:16])
    for s in first:
        home[s] = chip_swap(home[s], s)
    sign, held = lax.optimization_barrier((sign, held))
    for s, v in zip(second, held):
        home[s] = chip_swap(v, s)

    out = None
    for i in [*pairs[chips // 4 + 1 :], *pairs[: chips // 4 + 1]]:
        out = place_pair(tables[i], home[2 * i], home[2 * i + 1], out, divergence.shape, rows)
    return out


def solution(mesh):
    return jax.shard_map(
        local,
        mesh=mesh,
        in_specs=(P("wn", "tile", None), P("wn", None), P("wn"), P("wn"), P(), P("tile", None)),
        out_specs=P("wn", "tile", None),
        check_vma=False,
    )
```

```python
import functools
import math

import jax
import jax.numpy as jnp
from jax import lax
from jax.experimental import pallas as pl
from jax.experimental.pallas import tpu as pltpu
from jax.sharding import PartitionSpec as P

SWEEPS = 4
HALO = SWEEPS - 1
TAIL = 16
CHUNKS = 2
MIB = 1024 * 1024
F32, BF16 = jnp.float32, jnp.bfloat16


def params(mib):
    return pltpu.CompilerParams(vmem_limit_bytes=mib * MIB)


def cost(flops, nbytes):
    return pl.CostEstimate(flops=int(flops), bytes_accessed=int(nbytes), transcendentals=0)


LATE = pl.CostEstimate(flops=40_000_000_000, bytes_accessed=0, transcendentals=0)


def scale_body(table, w_ref, e_ref, x_ref, *o_refs):
    pairs = len(o_refs) // 2
    rows = x_ref.shape[1] // 2
    wide = x_ref.shape[2]
    w = w_ref[...]
    for i in range(pairs):

        @pl.when(pl.program_id(0) == i)
        def _(i=i):
            swap = table[pairs + i] != 0
            a_ref, b_ref = o_refs[2 * i], o_refs[2 * i + 1]
            for r in range(rows):
                low = (x_ref[:, r, :] * w).astype(BF16).T
                high = (x_ref[:, rows + r, :] * w).astype(BF16).T
                a_ref[r * wide : (r + 1) * wide, :] = jnp.where(swap, high, low)
                b_ref[r * wide : (r + 1) * wide, :] = jnp.where(swap, low, high)
            for ref in (a_ref, b_ref):
                ref[rows * wide : rows * wide + TAIL, :] = e_ref[...]
                if ref.shape[0] > rows * wide + TAIL:
                    ref[rows * wide + TAIL :, :] = e_ref[...]


def scale(table, weight, extra, divergence, chips, longer):
    planes, width, wide = divergence.shape
    rows, pairs = width // chips, chips // 2
    tall = rows * wide + extra.shape[0]
    return pl.pallas_call(
        scale_body,
        grid_spec=pltpu.PrefetchScalarGridSpec(
            num_scalar_prefetch=1,
            grid=(pairs,),
            in_specs=[
                pl.BlockSpec((planes, 1), lambda i, t: (0, 0)),
                pl.BlockSpec(extra.shape, lambda i, t: (0, 0)),
                pl.BlockSpec((planes, 2 * rows, wide), lambda i, t: (0, t[i], 0)),
            ],
            out_specs=[pl.BlockSpec(memory_space=pltpu.VMEM)] * chips,
        ),
        out_shape=[jax.ShapeDtypeStruct((tall + TAIL * (s in longer), planes), BF16) for s in range(chips)],
        compiler_params=params(12),
        cost_estimate=cost(planes * width * wide, planes * width * wide * 6),
    )(table, weight, extra, divergence)


def place_body(table, *refs):
    a_ref, b_ref, o_ref = refs[0], refs[1], refs[-1]
    rows = o_ref.shape[1] // 2
    wide = o_ref.shape[2]
    swap = table[1] != 0
    for r in range(rows):
        a = a_ref[r * wide : (r + 1) * wide, :]
        b = b_ref[r * wide : (r + 1) * wide, :]
        o_ref[:, r, :] = jnp.where(swap, b, a).T.astype(F32)
        o_ref[:, rows + r, :] = jnp.where(swap, a, b).T.astype(F32)


def place_pair(table, a, b, out, shape, rows):
    planes, _, wide = shape
    spec = pl.BlockSpec((rows * wide, planes), lambda i, t: (0, 0))
    ins, specs, alias = [a, b], [spec, spec], {}
    if out is not None:
        ins.append(out)
        specs.append(pl.BlockSpec(memory_space=pl.ANY))
        alias = {3: 0}
    return pl.pallas_call(
        place_body,
        grid_spec=pltpu.PrefetchScalarGridSpec(
            num_scalar_prefetch=1,
            grid=(1,),
            in_specs=specs,
            out_specs=pl.BlockSpec((planes, 2 * rows, wide), lambda i, t: (0, t[0], 0)),
        ),
        out_shape=jax.ShapeDtypeStruct(shape, F32),
        input_output_aliases=alias,
        compiler_params=params(12),
        cost_estimate=cost(planes * rows * wide * 2, planes * rows * wide * 12),
    )(table, *ins)


def run_copies(copies, sem):
    handles = [pltpu.make_async_copy(p, q, sem.at[k]) for k, (p, q) in enumerate(copies)]
    for h in handles:
        h.start()
    for h in handles:
        h.wait()


def gather_body(blocks, *refs):
    x_refs, (o_ref, e_ref, sem) = refs[: len(blocks)], refs[-3:]
    cells, planes = o_ref.shape[-2], x_refs[0].shape[1]
    copies = []
    for ref, s in zip(x_refs, blocks):
        copies.append((ref.at[pl.ds(cells, TAIL), :], e_ref.at[s]))
        place = o_ref.at[s] if len(o_ref.shape) == 3 else o_ref.at[:, pl.ds(s * planes, planes)]
        copies.append((ref.at[pl.ds(0, cells), :], place))
    run_copies(copies, sem)


def gather(xs, blocks, cells, chips, held, mark):
    planes = xs[0].shape[1]
    out = [
        pltpu.VMEM((chips, cells, planes) if planes % 128 else (cells, chips * planes), BF16),
        pltpu.VMEM((chips, TAIL, planes), BF16),
    ]
    count = len(xs) + (len(held) if held else 0)
    return pl.pallas_call(
        functools.partial(gather_body, tuple(blocks)),
        in_specs=[pl.BlockSpec(memory_space=pltpu.VMEM)] * count,
        out_specs=[pl.BlockSpec(memory_space=pltpu.VMEM)] * 2,
        out_shape=out,
        input_output_aliases={len(xs): 0, len(xs) + 1: 1} if held else {},
        scratch_shapes=[pltpu.SemaphoreType.DMA((2 * len(xs),))],
        compiler_params=params(12),
        cost_estimate=mark,
    )(*xs, *(held or []))


def join_body(layout, planes, half_ref, *refs):
    b_refs, (out, sem) = refs[: len(layout)], refs[-2:]
    part = planes // 2
    half = half_ref[0]
    copies = []
    for ref, (kind, ids) in zip(b_refs, layout):
        for j, s in enumerate(ids):
            if kind == "whole":
                src, dst = ref, out.at[pl.ds(s * planes, planes), :]
            else:
                side = half if kind == "mine" else 1 - half
                start = pl.multiple_of(s * planes + side * part, part)
                src, dst = ref.at[pl.ds(j * part, part), :], out.at[pl.ds(start, part), :]
            copies.append((src, dst))
    run_copies(copies, sem)


def join(half, pieces, layout, planes, chips, held, mark):
    modes = pieces[0].shape[1]
    home = pl.BlockSpec(memory_space=pltpu.HBM)
    specs = [pl.BlockSpec(memory_space=pltpu.SMEM)] + [pl.BlockSpec(memory_space=pltpu.VMEM)] * len(pieces)
    ins, alias = list(pieces), {}
    if held is not None:
        alias = {1 + len(ins): 0}
        specs.append(home)
        ins.append(held)
    return pl.pallas_call(
        functools.partial(join_body, layout, planes),
        in_specs=specs,
        out_specs=home,
        out_shape=pltpu.HBM((chips * planes, modes), BF16),
        input_output_aliases=alias,
        scratch_shapes=[pltpu.SemaphoreType.DMA((sum(len(ids) for _, ids in layout),))],
        compiler_params=params(12),
        cost_estimate=mark,
    )(half, *ins)


def forward_body(table, x_ref, b_ref, *refs):
    x = x_ref[...]
    if len(x.shape) == 3:
        x = jnp.concatenate([x[k] for k in range(x.shape[0])], axis=1)
    total = jnp.dot(x, b_ref[...], preferred_element_type=F32)
    if len(refs) == 2:
        total = total + refs[0][...]
    refs[-1][...] = total.astype(refs[-1].dtype)


def forward(table, x, basis, modes, tile, theirs=None):
    cells, depth = x.shape[-2], basis.shape[0]
    extra = [] if theirs is None else [theirs]
    return pl.pallas_call(
        forward_body,
        grid_spec=pltpu.PrefetchScalarGridSpec(
            num_scalar_prefetch=1,
            grid=(modes // tile,),
            in_specs=[
                pl.BlockSpec(memory_space=pltpu.VMEM),
                pl.BlockSpec((depth, tile), lambda j, t: (0, t[0] + j)),
            ]
            + [pl.BlockSpec((cells, tile), lambda j, t: (0, j))] * len(extra),
            out_specs=pl.BlockSpec((cells, tile), lambda j, t: (0, j)),
        ),
        out_shape=jax.ShapeDtypeStruct((cells, modes), BF16 if extra else F32),
        compiler_params=params(16),
        cost_estimate=cost(2 * cells * depth * modes, 2 * cells * depth + 2 * depth * modes + 4 * cells * modes),
    )(table, x, basis, *extra)


def sweep_body(eigen_ref, fluid_ref, up_ref, own_ref, down_ref, o_ref, rhs, ua, ub):
    rows = own_ref.shape[0]
    ext = rows + 2 * HALO
    diag = eigen_ref[...] + 4.0
    spread = 4.0 / diag
    keep, gain = [], []
    for step in range(SWEEPS):
        omega = 1.0 / (1.0 + spread * math.cos(math.pi * (2 * step + 1) / (2 * SWEEPS)))
        keep.append(1.0 - omega)
        gain.append(omega / diag)

    for ref, first in ((up_ref, 0), (own_ref, HALO), (down_ref, HALO + rows)):
        for r in range(ref.shape[0]):
            s = ref[r].astype(F32)
            rhs[first + r] = s
            ua[first + r] = fluid_ref[first + r] * (gain[0] * s)
    src, dst = ua, ub
    for step in range(1, SWEEPS):
        for r in range(step, ext - step):
            c = src[r]
            wide = c.shape[0]
            beside = src[r - 1] + src[r + 1] + (pltpu.roll(c, 1, 0) + pltpu.roll(c, wide - 1, 0))
            new = fluid_ref[r] * (keep[step] * c + gain[step] * (rhs[r] + beside))
            if step == SWEEPS - 1:
                o_ref[r - HALO] = new.astype(BF16)
            else:
                dst[r] = new
        src, dst = dst, src


def sweep(eigen, fluid, up, own, down):
    rows, wide, modes = own.shape
    ext, lanes = rows + 2 * HALO, 128
    block = lambda n: pl.BlockSpec((n, wide, lanes), lambda j: (0, 0, j))
    return pl.pallas_call(
        sweep_body,
        grid=(modes // lanes,),
        in_specs=[
            pl.BlockSpec((1, lanes), lambda j: (0, j)),
            pl.BlockSpec((ext, wide, lanes), lambda j: (0, 0, 0)),
            block(HALO),
            block(rows),
            block(HALO),
        ],
        out_specs=block(rows),
        out_shape=jax.ShapeDtypeStruct((rows, wide, modes), BF16),
        scratch_shapes=[pltpu.VMEM((ext, wide, lanes), F32)] * 3,
        compiler_params=params(16),
        cost_estimate=cost(modes * wide * ext * 400, 4 * modes * wide * ext),
    )(eigen, fluid, up, own, down)


def inverse_body(tile, skip, based, table, *refs):
    outs = 2 if len(refs) and refs[-1].dtype == BF16 else 1
    o_refs, ins = refs[-outs:], refs[:-outs]
    base_ref = ins[-1] if based else None
    parts, b_ref = (ins[:-2], ins[-2]) if based else (ins[:-1], ins[-1])
    cells, wide = parts[0].shape

    def body(i, _):
        rows = pl.ds(pl.multiple_of(i * tile, tile), tile)
        total = None
        for k, part in enumerate(parts):
            cols = pl.ds(pl.multiple_of(table[skip + k] * wide, wide), wide)
            term = lax.dot_general(
                part[rows, :], b_ref[:, cols], (((1,), (1,)), ((), ())), preferred_element_type=F32
            )
            total = term if total is None else total + term
        if based:
            total = total + base_ref[rows, :]
        if outs == 1:
            o_refs[0][rows, :] = total
        else:
            planes = o_refs[0].shape[1]
            o_refs[0][rows, :] = total[:, :planes].astype(BF16)
            o_refs[1][rows, :] = total[:, planes:].astype(BF16)
        return 0

    lax.fori_loop(0, cells // tile, body, 0)


def inverse(table, parts, basis, pair, planes, skip=0, base=None, part_only=False):
    cells, wide = parts[0].shape
    modes = basis.shape[1]
    whole = pl.BlockSpec(memory_space=pltpu.VMEM)
    if part_only:
        out, out_specs = jax.ShapeDtypeStruct((cells, 2 * planes), F32), whole
    else:
        out, out_specs = [jax.ShapeDtypeStruct((cells, planes), BF16)] * 2, [whole] * 2
    extra = [] if base is None else [base]
    return pl.pallas_call(
        functools.partial(inverse_body, min(cells, 256), skip, base is not None),
        grid=(1,),
        in_specs=[pl.BlockSpec(memory_space=pltpu.SMEM)]
        + [whole] * len(parts)
        + [pl.BlockSpec((2 * planes, modes), lambda i: (pair, 0))]
        + [whole] * len(extra),
        out_specs=out_specs,
        out_shape=out,
        compiler_params=params(16),
        cost_estimate=cost(4 * cells * modes * planes, 2 * cells * modes + 4 * planes * modes),
    )(table, *parts, basis, *extra)


def local(divergence, basis, eigen, plane_level, spacing, solid):
    planes, width, wide = divergence.shape
    wn, tiles = lax.axis_size("wn"), lax.axis_size("tile")
    chips = wn // 2
    rows = width // chips
    cells = rows * wide
    modes = basis.shape[1]
    mine = modes // 2
    me, t = lax.axis_index("wn"), lax.axis_index("tile")
    core, chip = me % 2, me // 2
    z, y, odd = chip // 2, chip % 2, t % 2
    i32 = lambda *v: jnp.stack([jnp.asarray(x, jnp.int32) for x in v])

    flip = lambda s: [(i, i ^ (2 * s)) for i in range(wn)]
    chip_swap = lambda v, s: lax.ppermute(v, "wn", flip(s))
    core_swap = lambda v: lax.ppermute(v, "wn", [(i, i ^ 1) for i in range(wn)])
    tile_swap = lambda v: lax.ppermute(v, "tile", [(i, i ^ 1) for i in range(tiles)])

    def pair_table(i):
        pz = z ^ i
        block = jnp.where(odd == 0, pz, chips // 2 - 1 - pz)
        return i32(block, y ^ (pz % 2) ^ odd)

    tables = [pair_table(i) for i in range(chips // 2)]
    order = lambda g: (g // 2) * 2 + ((g % 2) ^ ((g // 2) % 2))

    def device(tt, g):
        return order(g if tt % 2 == 0 else chips - 1 - g)

    snake = [(tt, device(tt, g)) for tt in range(tiles) for g in range(chips)]
    onward = [
        ((qa * 2 + c) * tiles + ta, (qb * 2 + c) * tiles + tb)
        for (ta, qa), (tb, qb) in zip(snake, snake[1:] + snake[:1])
        for c in range(2)
    ]
    backward = [(b, a) for a, b in onward]

    onehot = (plane_level[:, None] == jnp.arange(spacing.shape[0], dtype=jnp.int32)[None, :]).astype(F32)
    weight = jnp.sum(onehot * spacing[None, :], axis=1)[:, None]

    sibling = core_swap(eigen)
    both = jnp.stack([jnp.where(core == 0, eigen, sibling), jnp.where(core == 0, sibling, eigen)])
    high = lax.reduce_precision(both, 8, 7)
    middle = lax.reduce_precision(both - high, 8, 7)
    low = both - high - middle
    extra = jnp.concatenate([high, middle, low, jnp.zeros((10, planes), F32)]).astype(BF16)

    inside = (1 - solid).astype(F32)
    edges = [
        lax.ppermute(inside[width - HALO :], "tile", [(i, (i + 1) % tiles) for i in range(tiles)]),
        lax.ppermute(inside[:HALO], "tile", [((i + 1) % tiles, i) for i in range(tiles)]),
    ]

    divergence = pltpu.with_memory_space_constraint(divergence, pltpu.HBM)
    blocks = [table[0] for table in tables] + [table[1] for table in tables]
    send = scale(i32(*blocks), weight, extra, divergence, chips, range(3 * chips // 4, chips))

    half = planes // 2
    far = chips // 2
    ids = tuple(range(2, chips, 2))
    odds = tuple(range(1, chips, 2))
    small = cost(0, 1 << 20)

    own = lax.dynamic_slice_in_dim(basis, odd * half, half, 0)
    column = [chip_swap(own, s) for s in ids]
    beside = chip_swap(basis, 1)
    layout = (("whole", (0,)), *[("mine", (s,)) for s in ids], ("whole", (1,)))
    full = join(i32(odd), [basis, *column, beside], layout, planes, chips, None, LATE)
    column, beside, full, send, edges = lax.optimization_barrier((column, beside, full, send, edges))

    held = jnp.concatenate(column)
    over_y, over_x = chip_swap(held, 1), tile_swap(held)
    evens = list(range(far, far + far // 2))
    x = gather([send[0], *[chip_swap(send[s], s) for s in evens]], [0, *evens], cells, chips, None, LATE)
    over_y, over_x, x, send = lax.optimization_barrier((over_y, over_x, x, send))

    corner = tile_swap(over_y)
    full = join(i32(odd), [over_y, over_x], (("mine", odds[1:]), ("other", ids)), planes, chips, full, small)
    last, nearby = list(range(far + far // 2, chips)), list(range(1, far))
    final = [chip_swap(send[s], s) for s in last]
    close = [chip_swap(send[s], s) for s in nearby]
    x = gather([*final, *close], [*last, *nearby], cells, chips, x, LATE)
    corner, x = lax.optimization_barrier((corner, x))
    full = join(i32(odd), [corner], (("other", odds[1:]),), planes, chips, full, small)
    x, tails = x

    ring = jnp.concatenate([edges[0], inside, edges[1]])
    e = 2 * z + (y ^ (z % 2))
    g = jnp.where(odd == 0, e, chips - 1 - e)
    fluid = lax.dynamic_slice_in_dim(ring, g * rows, rows + 2 * HALO, 0)
    fluid = jnp.broadcast_to(fluid[:, :, None], fluid.shape + (128,))

    tails = tails.astype(F32)
    values = tails[:, 0:2] + tails[:, 2:4] + tails[:, 4:6]
    want = (core * (chips // 2) + jnp.arange(chips // 2, dtype=jnp.int32)) ^ chip
    pick = want[:, None] == jnp.arange(chips, dtype=jnp.int32)[None, :]
    eigens = jnp.sum(jnp.where(pick[:, :, None, None], values[None], 0.0), axis=1).reshape(1, mine)

    size = mine // CHUNKS
    tile = min(256, size)
    per = size // tile
    stored = pltpu.with_memory_space_constraint(full, pltpu.HBM)
    halos, solved, theirs = [], [], []
    mark = None
    for j in range(CHUNKS):
        start = i32(((1 - core) * CHUNKS + j) * per)
        if mark is not None:
            start, mark = lax.optimization_barrier((start, mark))
        mark = forward(start, x, stored, size, tile)
        theirs.append(core_swap(mark))
    for j in range(CHUNKS):
        start = i32((core * CHUNKS + j) * per)
        start, mark = lax.optimization_barrier((start, mark))
        mark = forward(start, x, stored, size, tile, theirs[j])
        spectral = mark.reshape(rows, wide, size)
        up = lax.ppermute(spectral[rows - HALO :], ("wn", "tile"), onward)
        down = lax.ppermute(spectral[:HALO], ("wn", "tile"), backward)
        halos.append((up, spectral, down))
    others = []
    for j in range(CHUNKS):
        up, spectral, down = halos[j]
        u = sweep(eigens[:, j * size : (j + 1) * size], fluid, up, spectral, down).reshape(cells, size)
        solved.append(u)
        others.append(core_swap(u))

    columns = i32(
        *[core * CHUNKS + j for j in range(CHUNKS)], *[(1 - core) * CHUNKS + j for j in range(CHUNKS)]
    )
    home = [None] * chips
    pairs = list(range(chips // 2))
    ready = [*solved, *others[:-1]]
    begun = inverse(columns, ready, full, pairs[-1], planes, 0, None, True)
    ended = inverse(columns, others[-1:], full, pairs[-1], planes, len(ready), begun)
    home[2 * pairs[-1]], home[2 * pairs[-1] + 1] = ended
    for i in reversed(pairs[:-1]):
        home[2 * i], home[2 * i + 1] = inverse(columns, solved + others, full, i, planes)
    first = [s for i in reversed(pairs[chips // 4 + 1 :]) for s in (2 * i + 1, 2 * i)]
    second = [s for i in reversed(pairs[: chips // 4 + 1]) for s in (2 * i + 1, 2 * i) if s]
    held = [home[s] for s in second]
    sign = core_swap(home[first[0]][:16])
    for s in first:
        home[s] = chip_swap(home[s], s)
    sign, held = lax.optimization_barrier((sign, held))
    for s, v in zip(second, held):
        home[s] = chip_swap(v, s)

    out = None
    for i in [*pairs[chips // 4 + 1 :], *pairs[: chips // 4 + 1]]:
        out = place_pair(tables[i], home[2 * i], home[2 * i + 1], out, divergence.shape, rows)
    return out


def solution(mesh):
    return jax.shard_map(
        local,
        mesh=mesh,
        in_specs=(P("wn", "tile", None), P("wn", None), P("wn"), P("wn"), P(), P("tile", None)),
        out_specs=P("wn", "tile", None),
        check_vma=False,
    )
```

```python
import functools
import math

import jax
import jax.numpy as jnp
from jax import lax
from jax.experimental import pallas as pl
from jax.experimental.pallas import tpu as pltpu
from jax.sharding import PartitionSpec as P

SWEEPS = 4
HALO = SWEEPS - 1
TAIL = 16
CHUNKS = 2
MIB = 1024 * 1024
F32, BF16 = jnp.float32, jnp.bfloat16


def params(mib):
    return pltpu.CompilerParams(vmem_limit_bytes=mib * MIB)


def cost(flops, nbytes):
    return pl.CostEstimate(flops=int(flops), bytes_accessed=int(nbytes), transcendentals=0)


LATE = pl.CostEstimate(flops=40_000_000_000, bytes_accessed=0, transcendentals=0)


def scale_body(table, w_ref, e_ref, x_ref, *o_refs):
    pairs = len(o_refs) // 2
    rows = x_ref.shape[1] // 2
    wide = x_ref.shape[2]
    w = w_ref[...]
    for i in range(pairs):

        @pl.when(pl.program_id(0) == i)
        def _(i=i):
            swap = table[pairs + i] != 0
            a_ref, b_ref = o_refs[2 * i], o_refs[2 * i + 1]
            for r in range(rows):
                low = (x_ref[:, r, :] * w).astype(BF16).T
                high = (x_ref[:, rows + r, :] * w).astype(BF16).T
                a_ref[r * wide : (r + 1) * wide, :] = jnp.where(swap, high, low)
                b_ref[r * wide : (r + 1) * wide, :] = jnp.where(swap, low, high)
            for ref in (a_ref, b_ref):
                ref[rows * wide : rows * wide + TAIL, :] = e_ref[...]
                if ref.shape[0] > rows * wide + TAIL:
                    ref[rows * wide + TAIL :, :] = e_ref[...]


def scale(table, weight, extra, divergence, chips, longer):
    planes, width, wide = divergence.shape
    rows, pairs = width // chips, chips // 2
    tall = rows * wide + extra.shape[0]
    return pl.pallas_call(
        scale_body,
        grid_spec=pltpu.PrefetchScalarGridSpec(
            num_scalar_prefetch=1,
            grid=(pairs,),
            in_specs=[
                pl.BlockSpec((planes, 1), lambda i, t: (0, 0)),
                pl.BlockSpec(extra.shape, lambda i, t: (0, 0)),
                pl.BlockSpec((planes, 2 * rows, wide), lambda i, t: (0, t[i], 0)),
            ],
            out_specs=[pl.BlockSpec(memory_space=pltpu.VMEM)] * chips,
        ),
        out_shape=[jax.ShapeDtypeStruct((tall + TAIL * (s in longer), planes), BF16) for s in range(chips)],
        compiler_params=params(12),
        cost_estimate=cost(planes * width * wide, planes * width * wide * 6),
    )(table, weight, extra, divergence)


def place_body(table, *refs):
    a_ref, b_ref, o_ref = refs[0], refs[1], refs[-1]
    rows = o_ref.shape[1] // 2
    wide = o_ref.shape[2]
    swap = table[1] != 0
    for r in range(rows):
        a = a_ref[r * wide : (r + 1) * wide, :]
        b = b_ref[r * wide : (r + 1) * wide, :]
        o_ref[:, r, :] = jnp.where(swap, b, a).T.astype(F32)
        o_ref[:, rows + r, :] = jnp.where(swap, a, b).T.astype(F32)


def place_pair(table, a, b, out, shape, rows):
    planes, _, wide = shape
    spec = pl.BlockSpec((rows * wide, planes), lambda i, t: (0, 0))
    ins, specs, alias = [a, b], [spec, spec], {}
    if out is not None:
        ins.append(out)
        specs.append(pl.BlockSpec(memory_space=pl.ANY))
        alias = {3: 0}
    return pl.pallas_call(
        place_body,
        grid_spec=pltpu.PrefetchScalarGridSpec(
            num_scalar_prefetch=1,
            grid=(1,),
            in_specs=specs,
            out_specs=pl.BlockSpec((planes, 2 * rows, wide), lambda i, t: (0, t[0], 0)),
        ),
        out_shape=jax.ShapeDtypeStruct(shape, F32),
        input_output_aliases=alias,
        compiler_params=params(12),
        cost_estimate=cost(planes * rows * wide * 2, planes * rows * wide * 12),
    )(table, *ins)


def run_copies(copies, sem):
    handles = [pltpu.make_async_copy(p, q, sem.at[k]) for k, (p, q) in enumerate(copies)]
    for h in handles:
        h.start()
    for h in handles:
        h.wait()


def gather_body(blocks, *refs):
    x_refs, (o_ref, e_ref, sem) = refs[: len(blocks)], refs[-3:]
    cells, planes = o_ref.shape[-2], x_refs[0].shape[1]
    copies = []
    for ref, s in zip(x_refs, blocks):
        copies.append((ref.at[pl.ds(cells, TAIL), :], e_ref.at[s]))
        place = o_ref.at[s] if len(o_ref.shape) == 3 else o_ref.at[:, pl.ds(s * planes, planes)]
        copies.append((ref.at[pl.ds(0, cells), :], place))
    run_copies(copies, sem)


def gather(xs, blocks, cells, chips, held, mark):
    planes = xs[0].shape[1]
    out = [
        pltpu.VMEM((chips, cells, planes) if planes % 128 else (cells, chips * planes), BF16),
        pltpu.VMEM((chips, TAIL, planes), BF16),
    ]
    count = len(xs) + (len(held) if held else 0)
    return pl.pallas_call(
        functools.partial(gather_body, tuple(blocks)),
        in_specs=[pl.BlockSpec(memory_space=pltpu.VMEM)] * count,
        out_specs=[pl.BlockSpec(memory_space=pltpu.VMEM)] * 2,
        out_shape=out,
        input_output_aliases={len(xs): 0, len(xs) + 1: 1} if held else {},
        scratch_shapes=[pltpu.SemaphoreType.DMA((2 * len(xs),))],
        compiler_params=params(12),
        cost_estimate=mark,
    )(*xs, *(held or []))


def join_body(layout, planes, half_ref, *refs):
    b_refs, (out, sem) = refs[: len(layout)], refs[-2:]
    part = planes // 2
    half = half_ref[0]
    copies = []
    for ref, (kind, ids) in zip(b_refs, layout):
        for j, s in enumerate(ids):
            if kind == "whole":
                src, dst = ref, out.at[pl.ds(s * planes, planes), :]
            else:
                side = half if kind == "mine" else 1 - half
                start = pl.multiple_of(s * planes + side * part, part)
                src, dst = ref.at[pl.ds(j * part, part), :], out.at[pl.ds(start, part), :]
            copies.append((src, dst))
    run_copies(copies, sem)


def join(half, pieces, layout, planes, chips, held, mark):
    modes = pieces[0].shape[1]
    home = pl.BlockSpec(memory_space=pltpu.HBM)
    specs = [pl.BlockSpec(memory_space=pltpu.SMEM)] + [pl.BlockSpec(memory_space=pltpu.VMEM)] * len(pieces)
    ins, alias = list(pieces), {}
    if held is not None:
        alias = {1 + len(ins): 0}
        specs.append(home)
        ins.append(held)
    return pl.pallas_call(
        functools.partial(join_body, layout, planes),
        in_specs=specs,
        out_specs=home,
        out_shape=pltpu.HBM((chips * planes, modes), BF16),
        input_output_aliases=alias,
        scratch_shapes=[pltpu.SemaphoreType.DMA((sum(len(ids) for _, ids in layout),))],
        compiler_params=params(12),
        cost_estimate=mark,
    )(half, *ins)


def forward_body(table, x_ref, b_ref, *refs):
    x = x_ref[...]
    if len(x.shape) == 3:
        x = jnp.concatenate([x[k] for k in range(x.shape[0])], axis=1)
    total = jnp.dot(x, b_ref[...], preferred_element_type=F32)
    if len(refs) == 2:
        total = total + refs[0][...]
    refs[-1][...] = total.astype(refs[-1].dtype)


def forward(table, x, basis, modes, tile, theirs=None):
    cells, depth = x.shape[-2], basis.shape[0]
    extra = [] if theirs is None else [theirs]
    return pl.pallas_call(
        forward_body,
        grid_spec=pltpu.PrefetchScalarGridSpec(
            num_scalar_prefetch=1,
            grid=(modes // tile,),
            in_specs=[
                pl.BlockSpec(memory_space=pltpu.VMEM),
                pl.BlockSpec((depth, tile), lambda j, t: (0, t[0] + j)),
            ]
            + [pl.BlockSpec((cells, tile), lambda j, t: (0, j))] * len(extra),
            out_specs=pl.BlockSpec((cells, tile), lambda j, t: (0, j)),
        ),
        out_shape=jax.ShapeDtypeStruct((cells, modes), BF16 if extra else F32),
        compiler_params=params(16),
        cost_estimate=cost(2 * cells * depth * modes, 2 * cells * depth + 2 * depth * modes + 4 * cells * modes),
    )(table, x, basis, *extra)


def sweep_body(eigen_ref, fluid_ref, up_ref, own_ref, down_ref, o_ref, rhs, ua, ub):
    rows = own_ref.shape[0]
    ext = rows + 2 * HALO
    diag = eigen_ref[...] + 4.0
    spread = 4.0 / diag
    keep, gain = [], []
    for step in range(SWEEPS):
        omega = 1.0 / (1.0 + spread * math.cos(math.pi * (2 * step + 1) / (2 * SWEEPS)))
        keep.append(1.0 - omega)
        gain.append(omega / diag)

    for ref, first in ((up_ref, 0), (own_ref, HALO), (down_ref, HALO + rows)):
        for r in range(ref.shape[0]):
            s = ref[r].astype(F32)
            rhs[first + r] = s
            ua[first + r] = fluid_ref[first + r] * (gain[0] * s)
    src, dst = ua, ub
    for step in range(1, SWEEPS):
        for r in range(step, ext - step):
            c = src[r]
            wide = c.shape[0]
            beside = src[r - 1] + src[r + 1] + (pltpu.roll(c, 1, 0) + pltpu.roll(c, wide - 1, 0))
            new = fluid_ref[r] * (keep[step] * c + gain[step] * (rhs[r] + beside))
            if step == SWEEPS - 1:
                o_ref[r - HALO] = new.astype(BF16)
            else:
                dst[r] = new
        src, dst = dst, src


def sweep(eigen, fluid, up, own, down):
    rows, wide, modes = own.shape
    ext, lanes = rows + 2 * HALO, 128
    block = lambda n: pl.BlockSpec((n, wide, lanes), lambda j: (0, 0, j))
    return pl.pallas_call(
        sweep_body,
        grid=(modes // lanes,),
        in_specs=[
            pl.BlockSpec((1, lanes), lambda j: (0, j)),
            pl.BlockSpec((ext, wide, lanes), lambda j: (0, 0, 0)),
            block(HALO),
            block(rows),
            block(HALO),
        ],
        out_specs=block(rows),
        out_shape=jax.ShapeDtypeStruct((rows, wide, modes), BF16),
        scratch_shapes=[pltpu.VMEM((ext, wide, lanes), F32)] * 3,
        compiler_params=params(16),
        cost_estimate=cost(modes * wide * ext * 400, 4 * modes * wide * ext),
    )(eigen, fluid, up, own, down)


def inverse_body(tile, skip, based, table, *refs):
    outs = 2 if len(refs) and refs[-1].dtype == BF16 else 1
    o_refs, ins = refs[-outs:], refs[:-outs]
    base_ref = ins[-1] if based else None
    parts, b_ref = (ins[:-2], ins[-2]) if based else (ins[:-1], ins[-1])
    cells, wide = parts[0].shape

    def body(i, _):
        rows = pl.ds(pl.multiple_of(i * tile, tile), tile)
        total = None
        for k, part in enumerate(parts):
            cols = pl.ds(pl.multiple_of(table[skip + k] * wide, wide), wide)
            term = lax.dot_general(
                part[rows, :], b_ref[:, cols], (((1,), (1,)), ((), ())), preferred_element_type=F32
            )
            total = term if total is None else total + term
        if based:
            total = total + base_ref[rows, :]
        if outs == 1:
            o_refs[0][rows, :] = total
        else:
            planes = o_refs[0].shape[1]
            o_refs[0][rows, :] = total[:, :planes].astype(BF16)
            o_refs[1][rows, :] = total[:, planes:].astype(BF16)
        return 0

    lax.fori_loop(0, cells // tile, body, 0)


def inverse(table, parts, basis, pair, planes, skip=0, base=None, part_only=False):
    cells, wide = parts[0].shape
    modes = basis.shape[1]
    whole = pl.BlockSpec(memory_space=pltpu.VMEM)
    if part_only:
        out, out_specs = jax.ShapeDtypeStruct((cells, 2 * planes), F32), whole
    else:
        out, out_specs = [jax.ShapeDtypeStruct((cells, planes), BF16)] * 2, [whole] * 2
    extra = [] if base is None else [base]
    return pl.pallas_call(
        functools.partial(inverse_body, min(cells, 256), skip, base is not None),
        grid=(1,),
        in_specs=[pl.BlockSpec(memory_space=pltpu.SMEM)]
        + [whole] * len(parts)
        + [pl.BlockSpec((2 * planes, modes), lambda i: (pair, 0))]
        + [whole] * len(extra),
        out_specs=out_specs,
        out_shape=out,
        compiler_params=params(16),
        cost_estimate=cost(4 * cells * modes * planes, 2 * cells * modes + 4 * planes * modes),
    )(table, *parts, basis, *extra)


def local(divergence, basis, eigen, plane_level, spacing, solid):
    planes, width, wide = divergence.shape
    wn, tiles = lax.axis_size("wn"), lax.axis_size("tile")
    chips = wn // 2
    rows = width // chips
    cells = rows * wide
    modes = basis.shape[1]
    mine = modes // 2
    me, t = lax.axis_index("wn"), lax.axis_index("tile")
    core, chip = me % 2, me // 2
    z, y, odd = chip // 2, chip % 2, t % 2
    i32 = lambda *v: jnp.stack([jnp.asarray(x, jnp.int32) for x in v])

    flip = lambda s: [(i, i ^ (2 * s)) for i in range(wn)]
    chip_swap = lambda v, s: lax.ppermute(v, "wn", flip(s))
    core_swap = lambda v: lax.ppermute(v, "wn", [(i, i ^ 1) for i in range(wn)])
    tile_swap = lambda v: lax.ppermute(v, "tile", [(i, i ^ 1) for i in range(tiles)])

    def pair_table(i):
        pz = z ^ i
        block = jnp.where(odd == 0, pz, chips // 2 - 1 - pz)
        return i32(block, y ^ (pz % 2) ^ odd)

    tables = [pair_table(i) for i in range(chips // 2)]
    order = lambda g: (g // 2) * 2 + ((g % 2) ^ ((g // 2) % 2))

    def device(tt, g):
        return order(g if tt % 2 == 0 else chips - 1 - g)

    snake = [(tt, device(tt, g)) for tt in range(tiles) for g in range(chips)]
    onward = [
        ((qa * 2 + c) * tiles + ta, (qb * 2 + c) * tiles + tb)
        for (ta, qa), (tb, qb) in zip(snake, snake[1:] + snake[:1])
        for c in range(2)
    ]
    backward = [(b, a) for a, b in onward]

    onehot = (plane_level[:, None] == jnp.arange(spacing.shape[0], dtype=jnp.int32)[None, :]).astype(F32)
    weight = jnp.sum(onehot * spacing[None, :], axis=1)[:, None]

    sibling = core_swap(eigen)
    both = jnp.stack([jnp.where(core == 0, eigen, sibling), jnp.where(core == 0, sibling, eigen)])
    high = lax.reduce_precision(both, 8, 7)
    middle = lax.reduce_precision(both - high, 8, 7)
    low = both - high - middle
    extra = jnp.concatenate([high, middle, low, jnp.zeros((10, planes), F32)]).astype(BF16)

    inside = (1 - solid).astype(F32)
    edges = [
        lax.ppermute(inside[width - HALO :], "tile", [(i, (i + 1) % tiles) for i in range(tiles)]),
        lax.ppermute(inside[:HALO], "tile", [((i + 1) % tiles, i) for i in range(tiles)]),
    ]

    divergence = pltpu.with_memory_space_constraint(divergence, pltpu.HBM)
    blocks = [table[0] for table in tables] + [table[1] for table in tables]
    send = scale(i32(*blocks), weight, extra, divergence, chips, range(3 * chips // 4, chips))

    half = planes // 2
    far = chips // 2
    ids = tuple(range(2, chips, 2))
    odds = tuple(range(1, chips, 2))
    small = cost(0, 1 << 20)

    own = lax.dynamic_slice_in_dim(basis, odd * half, half, 0)
    column = [chip_swap(own, s) for s in ids]
    beside = chip_swap(basis, 1)
    layout = (("whole", (0,)), *[("mine", (s,)) for s in ids], ("whole", (1,)))
    full = join(i32(odd), [basis, *column, beside], layout, planes, chips, None, LATE)
    column, beside, full, send, edges = lax.optimization_barrier((column, beside, full, send, edges))

    held = jnp.concatenate(column)
    over_y, over_x = chip_swap(held, 1), tile_swap(held)
    evens = list(range(far, far + far // 2))
    x = gather([send[0], *[chip_swap(send[s], s) for s in evens]], [0, *evens], cells, chips, None, LATE)
    over_y, over_x, x, send = lax.optimization_barrier((over_y, over_x, x, send))

    corner = tile_swap(over_y)
    full = join(i32(odd), [over_y, over_x], (("mine", odds[1:]), ("other", ids)), planes, chips, full, small)
    last, nearby = list(range(far + far // 2, chips)), list(range(1, far))
    final = [chip_swap(send[s], s) for s in last]
    close = [chip_swap(send[s], s) for s in nearby]
    x = gather([*final, *close], [*last, *nearby], cells, chips, x, LATE)
    corner, x = lax.optimization_barrier((corner, x))
    full = join(i32(odd), [corner], (("other", odds[1:]),), planes, chips, full, small)
    x, tails = x

    ring = jnp.concatenate([edges[0], inside, edges[1]])
    e = 2 * z + (y ^ (z % 2))
    g = jnp.where(odd == 0, e, chips - 1 - e)
    fluid = lax.dynamic_slice_in_dim(ring, g * rows, rows + 2 * HALO, 0)
    fluid = jnp.broadcast_to(fluid[:, :, None], fluid.shape + (128,))

    tails = tails.astype(F32)
    values = tails[:, 0:2] + tails[:, 2:4] + tails[:, 4:6]
    want = (core * (chips // 2) + jnp.arange(chips // 2, dtype=jnp.int32)) ^ chip
    pick = want[:, None] == jnp.arange(chips, dtype=jnp.int32)[None, :]
    eigens = jnp.sum(jnp.where(pick[:, :, None, None], values[None], 0.0), axis=1).reshape(1, mine)

    size = mine // CHUNKS
    tile = min(256, size)
    per = size // tile
    stored = pltpu.with_memory_space_constraint(full, pltpu.HBM)
    halos, solved, theirs = [], [], []
    mark = None
    for j in range(CHUNKS):
        start = i32(((1 - core) * CHUNKS + j) * per)
        if mark is not None:
            start, mark = lax.optimization_barrier((start, mark))
        mark = forward(start, x, stored, size, tile)
        theirs.append(core_swap(mark))
    for j in range(CHUNKS):
        start = i32((core * CHUNKS + j) * per)
        start, mark = lax.optimization_barrier((start, mark))
        mark = forward(start, x, stored, size, tile, theirs[j])
        spectral = mark.reshape(rows, wide, size)
        up = lax.ppermute(spectral[rows - HALO :], ("wn", "tile"), onward)
        down = lax.ppermute(spectral[:HALO], ("wn", "tile"), backward)
        halos.append((up, spectral, down))
    others = []
    for j in range(CHUNKS):
        up, spectral, down = halos[j]
        u = sweep(eigens[:, j * size : (j + 1) * size], fluid, up, spectral, down).reshape(cells, size)
        solved.append(u)
        others.append(core_swap(u))

    columns = i32(
        *[core * CHUNKS + j for j in range(CHUNKS)], *[(1 - core) * CHUNKS + j for j in range(CHUNKS)]
    )
    home = [None] * chips
    pairs = list(range(chips // 2))
    ready = [*solved, *others[:-1]]
    begun = inverse(columns, ready, full, pairs[-1], planes, 0, None, True)
    for i in reversed(pairs):
        if i == pairs[-1]:
            a, b = inverse(columns, others[-1:], full, i, planes, len(ready), begun)
        else:
            a, b = inverse(columns, solved + others, full, i, planes)
        columns, a, b = lax.optimization_barrier((columns, a, b))
        home[2 * i], home[2 * i + 1] = a if i == 0 else chip_swap(a, 2 * i), chip_swap(b, 2 * i + 1)

    out = None
    for i in [*pairs[chips // 4 + 1 :], *pairs[: chips // 4 + 1]]:
        out = place_pair(tables[i], home[2 * i], home[2 * i + 1], out, divergence.shape, rows)
    return out


def solution(mesh):
    return jax.shard_map(
        local,
        mesh=mesh,
        in_specs=(P("wn", "tile", None), P("wn", None), P("wn"), P("wn"), P(), P("tile", None)),
        out_specs=P("wn", "tile", None),
        check_vma=False,
    )
```

```python
import functools
import math

import jax
import jax.numpy as jnp
from jax import lax
from jax.experimental import pallas as pl
from jax.experimental.pallas import tpu as pltpu
from jax.sharding import PartitionSpec as P

SWEEPS = 4
HALO = SWEEPS - 1
TAIL = 16
CHUNKS = 2
MIB = 1024 * 1024
F32, BF16 = jnp.float32, jnp.bfloat16


def params(mib):
    return pltpu.CompilerParams(vmem_limit_bytes=mib * MIB)


def cost(flops, nbytes):
    return pl.CostEstimate(flops=int(flops), bytes_accessed=int(nbytes), transcendentals=0)


LATE = pl.CostEstimate(flops=40_000_000_000, bytes_accessed=0, transcendentals=0)


def scale_body(table, w_ref, e_ref, x_ref, *o_refs):
    pairs = len(o_refs) // 2
    rows = x_ref.shape[1] // 2
    wide = x_ref.shape[2]
    w = w_ref[...]
    for i in range(pairs):

        @pl.when(pl.program_id(0) == i)
        def _(i=i):
            swap = table[pairs + i] != 0
            a_ref, b_ref = o_refs[2 * i], o_refs[2 * i + 1]
            for r in range(rows):
                low = (x_ref[:, r, :] * w).astype(BF16).T
                high = (x_ref[:, rows + r, :] * w).astype(BF16).T
                a_ref[r * wide : (r + 1) * wide, :] = jnp.where(swap, high, low)
                b_ref[r * wide : (r + 1) * wide, :] = jnp.where(swap, low, high)
            for ref in (a_ref, b_ref):
                ref[rows * wide : rows * wide + TAIL, :] = e_ref[...]
                if ref.shape[0] > rows * wide + TAIL:
                    ref[rows * wide + TAIL :, :] = e_ref[...]


def scale(table, weight, extra, divergence, chips, longer):
    planes, width, wide = divergence.shape
    rows, pairs = width // chips, chips // 2
    tall = rows * wide + extra.shape[0]
    return pl.pallas_call(
        scale_body,
        grid_spec=pltpu.PrefetchScalarGridSpec(
            num_scalar_prefetch=1,
            grid=(pairs,),
            in_specs=[
                pl.BlockSpec((planes, 1), lambda i, t: (0, 0)),
                pl.BlockSpec(extra.shape, lambda i, t: (0, 0)),
                pl.BlockSpec((planes, 2 * rows, wide), lambda i, t: (0, t[i], 0)),
            ],
            out_specs=[pl.BlockSpec(memory_space=pltpu.VMEM)] * chips,
        ),
        out_shape=[jax.ShapeDtypeStruct((tall + TAIL * (s in longer), planes), BF16) for s in range(chips)],
        compiler_params=params(12),
        cost_estimate=cost(planes * width * wide, planes * width * wide * 6),
    )(table, weight, extra, divergence)


def place_body(table, *refs):
    a_ref, b_ref, o_ref = refs[0], refs[1], refs[-1]
    rows = o_ref.shape[1] // 2
    wide = o_ref.shape[2]
    swap = table[1] != 0
    for r in range(rows):
        a = a_ref[r * wide : (r + 1) * wide, :]
        b = b_ref[r * wide : (r + 1) * wide, :]
        o_ref[:, r, :] = jnp.where(swap, b, a).T.astype(F32)
        o_ref[:, rows + r, :] = jnp.where(swap, a, b).T.astype(F32)


def place_pair(table, a, b, out, shape, rows):
    planes, _, wide = shape
    spec = pl.BlockSpec((rows * wide, planes), lambda i, t: (0, 0))
    ins, specs, alias = [a, b], [spec, spec], {}
    if out is not None:
        ins.append(out)
        specs.append(pl.BlockSpec(memory_space=pl.ANY))
        alias = {3: 0}
    return pl.pallas_call(
        place_body,
        grid_spec=pltpu.PrefetchScalarGridSpec(
            num_scalar_prefetch=1,
            grid=(1,),
            in_specs=specs,
            out_specs=pl.BlockSpec((planes, 2 * rows, wide), lambda i, t: (0, t[0], 0)),
        ),
        out_shape=jax.ShapeDtypeStruct(shape, F32),
        input_output_aliases=alias,
        compiler_params=params(12),
        cost_estimate=cost(planes * rows * wide * 2, planes * rows * wide * 12),
    )(table, *ins)


def run_copies(copies, sem):
    handles = [pltpu.make_async_copy(p, q, sem.at[k]) for k, (p, q) in enumerate(copies)]
    for h in handles:
        h.start()
    for h in handles:
        h.wait()


def gather_body(blocks, *refs):
    x_refs, (o_ref, e_ref, sem) = refs[: len(blocks)], refs[-3:]
    cells, planes = o_ref.shape[-2], x_refs[0].shape[1]
    copies = []
    for ref, s in zip(x_refs, blocks):
        copies.append((ref.at[pl.ds(cells, TAIL), :], e_ref.at[s]))
        place = o_ref.at[s] if len(o_ref.shape) == 3 else o_ref.at[:, pl.ds(s * planes, planes)]
        copies.append((ref.at[pl.ds(0, cells), :], place))
    run_copies(copies, sem)


def gather(xs, blocks, cells, chips, held, mark):
    planes = xs[0].shape[1]
    out = [
        pltpu.VMEM((chips, cells, planes) if planes % 128 else (cells, chips * planes), BF16),
        pltpu.VMEM((chips, TAIL, planes), BF16),
    ]
    count = len(xs) + (len(held) if held else 0)
    return pl.pallas_call(
        functools.partial(gather_body, tuple(blocks)),
        in_specs=[pl.BlockSpec(memory_space=pltpu.VMEM)] * count,
        out_specs=[pl.BlockSpec(memory_space=pltpu.VMEM)] * 2,
        out_shape=out,
        input_output_aliases={len(xs): 0, len(xs) + 1: 1} if held else {},
        scratch_shapes=[pltpu.SemaphoreType.DMA((2 * len(xs),))],
        compiler_params=params(12),
        cost_estimate=mark,
    )(*xs, *(held or []))


def join_body(layout, planes, half_ref, *refs):
    b_refs, (out, sem) = refs[: len(layout)], refs[-2:]
    part = planes // 2
    half = half_ref[0]
    copies = []
    for ref, (kind, ids) in zip(b_refs, layout):
        for j, s in enumerate(ids):
            if kind == "whole":
                src, dst = ref, out.at[pl.ds(s * planes, planes), :]
            else:
                side = half if kind == "mine" else 1 - half
                start = pl.multiple_of(s * planes + side * part, part)
                src, dst = ref.at[pl.ds(j * part, part), :], out.at[pl.ds(start, part), :]
            copies.append((src, dst))
    run_copies(copies, sem)


def join(half, pieces, layout, planes, chips, held, mark):
    modes = pieces[0].shape[1]
    home = pl.BlockSpec(memory_space=pltpu.HBM)
    specs = [pl.BlockSpec(memory_space=pltpu.SMEM)] + [pl.BlockSpec(memory_space=pltpu.VMEM)] * len(pieces)
    ins, alias = list(pieces), {}
    if held is not None:
        alias = {1 + len(ins): 0}
        specs.append(home)
        ins.append(held)
    return pl.pallas_call(
        functools.partial(join_body, layout, planes),
        in_specs=specs,
        out_specs=home,
        out_shape=pltpu.HBM((chips * planes, modes), BF16),
        input_output_aliases=alias,
        scratch_shapes=[pltpu.SemaphoreType.DMA((sum(len(ids) for _, ids in layout),))],
        compiler_params=params(12),
        cost_estimate=mark,
    )(half, *ins)


def forward_body(table, x_ref, b_ref, *refs):
    x = x_ref[...]
    if len(x.shape) == 3:
        x = jnp.concatenate([x[k] for k in range(x.shape[0])], axis=1)
    total = jnp.dot(x, b_ref[...], preferred_element_type=F32)
    if len(refs) == 2:
        total = total + refs[0][...]
    refs[-1][...] = total.astype(refs[-1].dtype)


def forward(table, x, basis, modes, tile, theirs=None):
    cells, depth = x.shape[-2], basis.shape[0]
    extra = [] if theirs is None else [theirs]
    return pl.pallas_call(
        forward_body,
        grid_spec=pltpu.PrefetchScalarGridSpec(
            num_scalar_prefetch=1,
            grid=(modes // tile,),
            in_specs=[
                pl.BlockSpec(memory_space=pltpu.VMEM),
                pl.BlockSpec((depth, tile), lambda j, t: (0, t[0] + j)),
            ]
            + [pl.BlockSpec((cells, tile), lambda j, t: (0, j))] * len(extra),
            out_specs=pl.BlockSpec((cells, tile), lambda j, t: (0, j)),
        ),
        out_shape=jax.ShapeDtypeStruct((cells, modes), BF16 if extra else F32),
        compiler_params=params(16),
        cost_estimate=cost(2 * cells * depth * modes, 2 * cells * depth + 2 * depth * modes + 4 * cells * modes),
    )(table, x, basis, *extra)


def sweep_body(eigen_ref, fluid_ref, up_ref, own_ref, down_ref, o_ref, rhs, ua, ub):
    rows = own_ref.shape[0]
    ext = rows + 2 * HALO
    diag = eigen_ref[...] + 4.0
    spread = 4.0 / diag
    keep, gain = [], []
    for step in range(SWEEPS):
        omega = 1.0 / (1.0 + spread * math.cos(math.pi * (2 * step + 1) / (2 * SWEEPS)))
        keep.append(1.0 - omega)
        gain.append(omega / diag)

    for ref, first in ((up_ref, 0), (own_ref, HALO), (down_ref, HALO + rows)):
        for r in range(ref.shape[0]):
            s = ref[r].astype(F32)
            rhs[first + r] = s
            ua[first + r] = fluid_ref[first + r] * (gain[0] * s)
    src, dst = ua, ub
    for step in range(1, SWEEPS):
        for r in range(step, ext - step):
            c = src[r]
            wide = c.shape[0]
            beside = src[r - 1] + src[r + 1] + (pltpu.roll(c, 1, 0) + pltpu.roll(c, wide - 1, 0))
            new = fluid_ref[r] * (keep[step] * c + gain[step] * (rhs[r] + beside))
            if step == SWEEPS - 1:
                o_ref[r - HALO] = new.astype(BF16)
            else:
                dst[r] = new
        src, dst = dst, src


def sweep(eigen, fluid, up, own, down):
    rows, wide, modes = own.shape
    ext, lanes = rows + 2 * HALO, 128
    block = lambda n: pl.BlockSpec((n, wide, lanes), lambda j: (0, 0, j))
    return pl.pallas_call(
        sweep_body,
        grid=(modes // lanes,),
        in_specs=[
            pl.BlockSpec((1, lanes), lambda j: (0, j)),
            pl.BlockSpec((ext, wide, lanes), lambda j: (0, 0, 0)),
            block(HALO),
            block(rows),
            block(HALO),
        ],
        out_specs=block(rows),
        out_shape=jax.ShapeDtypeStruct((rows, wide, modes), BF16),
        scratch_shapes=[pltpu.VMEM((ext, wide, lanes), F32)] * 3,
        compiler_params=params(16),
        cost_estimate=cost(modes * wide * ext * 400, 4 * modes * wide * ext),
    )(eigen, fluid, up, own, down)


def inverse_body(tile, skip, based, table, *refs):
    outs = 2 if len(refs) and refs[-1].dtype == BF16 else 1
    o_refs, ins = refs[-outs:], refs[:-outs]
    base_ref = ins[-1] if based else None
    parts, b_ref = (ins[:-2], ins[-2]) if based else (ins[:-1], ins[-1])
    cells, wide = parts[0].shape

    def body(i, _):
        rows = pl.ds(pl.multiple_of(i * tile, tile), tile)
        total = None
        for k, part in enumerate(parts):
            cols = pl.ds(pl.multiple_of(table[skip + k] * wide, wide), wide)
            term = lax.dot_general(
                part[rows, :], b_ref[:, cols], (((1,), (1,)), ((), ())), preferred_element_type=F32
            )
            total = term if total is None else total + term
        if based:
            total = total + base_ref[rows, :]
        if outs == 1:
            o_refs[0][rows, :] = total
        else:
            planes = o_refs[0].shape[1]
            o_refs[0][rows, :] = total[:, :planes].astype(BF16)
            o_refs[1][rows, :] = total[:, planes:].astype(BF16)
        return 0

    lax.fori_loop(0, cells // tile, body, 0)


def inverse(table, parts, basis, pair, planes, skip=0, base=None, part_only=False):
    cells, wide = parts[0].shape
    modes = basis.shape[1]
    whole = pl.BlockSpec(memory_space=pltpu.VMEM)
    if part_only:
        out, out_specs = jax.ShapeDtypeStruct((cells, 2 * planes), F32), whole
    else:
        out, out_specs = [jax.ShapeDtypeStruct((cells, planes), BF16)] * 2, [whole] * 2
    extra = [] if base is None else [base]
    return pl.pallas_call(
        functools.partial(inverse_body, min(cells, 256), skip, base is not None),
        grid=(1,),
        in_specs=[pl.BlockSpec(memory_space=pltpu.SMEM)]
        + [whole] * len(parts)
        + [pl.BlockSpec((2 * planes, modes), lambda i: (pair, 0))]
        + [whole] * len(extra),
        out_specs=out_specs,
        out_shape=out,
        compiler_params=params(16),
        cost_estimate=cost(4 * cells * modes * planes, 2 * cells * modes + 4 * planes * modes),
    )(table, *parts, basis, *extra)


def local(divergence, basis, eigen, plane_level, spacing, solid):
    planes, width, wide = divergence.shape
    wn, tiles = lax.axis_size("wn"), lax.axis_size("tile")
    chips = wn // 2
    rows = width // chips
    cells = rows * wide
    modes = basis.shape[1]
    mine = modes // 2
    me, t = lax.axis_index("wn"), lax.axis_index("tile")
    core, chip = me % 2, me // 2
    z, y, odd = chip // 2, chip % 2, t % 2
    i32 = lambda *v: jnp.stack([jnp.asarray(x, jnp.int32) for x in v])

    flip = lambda s: [(i, i ^ (2 * s)) for i in range(wn)]
    chip_swap = lambda v, s: lax.ppermute(v, "wn", flip(s))
    core_swap = lambda v: lax.ppermute(v, "wn", [(i, i ^ 1) for i in range(wn)])
    tile_swap = lambda v: lax.ppermute(v, "tile", [(i, i ^ 1) for i in range(tiles)])

    def pair_table(i):
        pz = z ^ i
        block = jnp.where(odd == 0, pz, chips // 2 - 1 - pz)
        return i32(block, y ^ (pz % 2) ^ odd)

    tables = [pair_table(i) for i in range(chips // 2)]
    order = lambda g: (g // 2) * 2 + ((g % 2) ^ ((g // 2) % 2))

    def device(tt, g):
        return order(g if tt % 2 == 0 else chips - 1 - g)

    snake = [(tt, device(tt, g)) for tt in range(tiles) for g in range(chips)]
    onward = [
        ((qa * 2 + c) * tiles + ta, (qb * 2 + c) * tiles + tb)
        for (ta, qa), (tb, qb) in zip(snake, snake[1:] + snake[:1])
        for c in range(2)
    ]
    backward = [(b, a) for a, b in onward]

    onehot = (plane_level[:, None] == jnp.arange(spacing.shape[0], dtype=jnp.int32)[None, :]).astype(F32)
    weight = jnp.sum(onehot * spacing[None, :], axis=1)[:, None]

    sibling = core_swap(eigen)
    both = jnp.stack([jnp.where(core == 0, eigen, sibling), jnp.where(core == 0, sibling, eigen)])
    high = lax.reduce_precision(both, 8, 7)
    middle = lax.reduce_precision(both - high, 8, 7)
    low = both - high - middle
    extra = jnp.concatenate([high, middle, low, jnp.zeros((10, planes), F32)]).astype(BF16)

    inside = (1 - solid).astype(F32)
    edges = [
        lax.ppermute(inside[width - HALO :], "tile", [(i, (i + 1) % tiles) for i in range(tiles)]),
        lax.ppermute(inside[:HALO], "tile", [((i + 1) % tiles, i) for i in range(tiles)]),
    ]

    divergence = pltpu.with_memory_space_constraint(divergence, pltpu.HBM)
    blocks = [table[0] for table in tables] + [table[1] for table in tables]
    send = scale(i32(*blocks), weight, extra, divergence, chips, range(3 * chips // 4, chips))

    half = planes // 2
    far = chips // 2
    ids = tuple(range(2, chips, 2))
    odds = tuple(range(1, chips, 2))
    small = cost(0, 1 << 20)

    own = lax.dynamic_slice_in_dim(basis, odd * half, half, 0)
    column = [chip_swap(own, s) for s in ids]
    beside = chip_swap(basis, 1)
    layout = (("whole", (0,)), *[("mine", (s,)) for s in ids], ("whole", (1,)))
    full = join(i32(odd), [basis, *column, beside], layout, planes, chips, None, LATE)
    column, beside, full, send, edges = lax.optimization_barrier((column, beside, full, send, edges))

    held = jnp.concatenate(column)
    over_y, over_x = chip_swap(held, 1), tile_swap(held)
    evens = [*range(far, far + far // 2), 2]
    x = gather([send[0], *[chip_swap(send[s], s) for s in evens]], [0, *evens], cells, chips, None, LATE)
    over_y, over_x, x, send = lax.optimization_barrier((over_y, over_x, x, send))

    corner = tile_swap(over_y)
    full = join(i32(odd), [over_y, over_x], (("mine", odds[1:]), ("other", ids)), planes, chips, full, small)
    last, nearby = list(range(far + far // 2, chips)), [1, *range(3, far)]
    final = [chip_swap(send[s], s) for s in last]
    close = [chip_swap(send[s], s) for s in nearby]
    x = gather([*final, *close], [*last, *nearby], cells, chips, x, LATE)
    corner, x = lax.optimization_barrier((corner, x))
    full = join(i32(odd), [corner], (("other", odds[1:]),), planes, chips, full, small)
    x, tails = x

    ring = jnp.concatenate([edges[0], inside, edges[1]])
    e = 2 * z + (y ^ (z % 2))
    g = jnp.where(odd == 0, e, chips - 1 - e)
    fluid = lax.dynamic_slice_in_dim(ring, g * rows, rows + 2 * HALO, 0)
    fluid = jnp.broadcast_to(fluid[:, :, None], fluid.shape + (128,))

    tails = tails.astype(F32)
    values = tails[:, 0:2] + tails[:, 2:4] + tails[:, 4:6]
    want = (core * (chips // 2) + jnp.arange(chips // 2, dtype=jnp.int32)) ^ chip
    pick = want[:, None] == jnp.arange(chips, dtype=jnp.int32)[None, :]
    eigens = jnp.sum(jnp.where(pick[:, :, None, None], values[None], 0.0), axis=1).reshape(1, mine)

    size = mine // CHUNKS
    tile = min(256, size)
    per = size // tile
    stored = pltpu.with_memory_space_constraint(full, pltpu.HBM)
    halos, solved, theirs = [], [], []
    mark = None
    for j in range(CHUNKS):
        start = i32(((1 - core) * CHUNKS + j) * per)
        if mark is not None:
            start, mark = lax.optimization_barrier((start, mark))
        mark = forward(start, x, stored, size, tile)
        theirs.append(core_swap(mark))
    for j in range(CHUNKS):
        start = i32((core * CHUNKS + j) * per)
        start, mark = lax.optimization_barrier((start, mark))
        mark = forward(start, x, stored, size, tile, theirs[j])
        spectral = mark.reshape(rows, wide, size)
        up = lax.ppermute(spectral[rows - HALO :], ("wn", "tile"), onward)
        down = lax.ppermute(spectral[:HALO], ("wn", "tile"), backward)
        halos.append((up, spectral, down))
    others = []
    for j in range(CHUNKS):
        up, spectral, down = halos[j]
        u = sweep(eigens[:, j * size : (j + 1) * size], fluid, up, spectral, down).reshape(cells, size)
        solved.append(u)
        others.append(core_swap(u))

    columns = i32(
        *[core * CHUNKS + j for j in range(CHUNKS)], *[(1 - core) * CHUNKS + j for j in range(CHUNKS)]
    )
    home = [None] * chips
    pairs = list(range(chips // 2))
    ready = [*solved, *others[:-1]]
    begun = inverse(columns, ready, full, pairs[-1], planes, 0, None, True)
    ended = inverse(columns, others[-1:], full, pairs[-1], planes, len(ready), begun)
    home[2 * pairs[-1]], home[2 * pairs[-1] + 1] = ended
    for i in reversed(pairs[:-1]):
        home[2 * i], home[2 * i + 1] = inverse(columns, solved + others, full, i, planes)
    first = [s for i in reversed(pairs[chips // 4 + 1 :]) for s in (2 * i + 1, 2 * i)]
    second = [s for i in reversed(pairs[: chips // 4 + 1]) for s in (2 * i + 1, 2 * i) if s]
    held = [home[s] for s in second]
    sign = core_swap(home[first[0]][:16])
    for s in first:
        home[s] = chip_swap(home[s], s)
    sign, held = lax.optimization_barrier((sign, held))
    for s, v in zip(second, held):
        home[s] = chip_swap(v, s)

    out = None
    for i in [*pairs[chips // 4 + 1 :], *pairs[: chips // 4 + 1]]:
        out = place_pair(tables[i], home[2 * i], home[2 * i + 1], out, divergence.shape, rows)
    return out


def solution(mesh):
    return jax.shard_map(
        local,
        mesh=mesh,
        in_specs=(P("wn", "tile", None), P("wn", None), P("wn"), P("wn"), P(), P("tile", None)),
        out_specs=P("wn", "tile", None),
        check_vma=False,
    )
```
